128 devices in a mesh: head: 8 (over x, z_lo), group: 16 (over y, z_hi, core).
Axes of the slice: x: 4, y: 4, z: 4 (z_hi: 2, z_lo: 2; z = z_hi * 2 + z_lo), core: 2. Of those that a mesh axis runs over, the one named last changes fastest.
Arguments:
- memory: float32 [128, 8, 256, 512], P('group', 'head'), may hold values from -6 to 6
- normalizer: float32 [128, 8, 256], P('group', 'head'), may hold values from -9 to 9
- queries: bfloat16 [4, 128, 8, 256], P(None, 'group', 'head'), may hold values from -6 to 6
- keys: bfloat16 [4, 128, 8, 256], P(None, 'group', 'head'), may hold values from -6 to 6
- values: bfloat16 [4, 128, 8, 512], P(None, 'group', 'head'), may hold values from -6 to 6
- igate: float32 [4, 128, 8], P(None, 'group', 'head'), may hold values from -3 to 1
- fgate: float32 [4, 128, 8], P(None, 'group', 'head'), may hold values from -2 to 4
- ogate: bfloat16 [4, 128, 8, 512], P(None, 'group', 'head'), may hold values from -6 to 6
- out_weight: bfloat16 [8, 512, 4096], P('head'), may hold values from -0.09375 to 0.09375
- tokens: bfloat16 [4, 128, 4096], P(None, 'group', 'head'), may hold values from -3 to 3
- active: int32 [128], P('group'), may hold values 0 or 1
- pair_mask: int32 [1], replicated, may hold values from 1 to 15
- swap_slots: int32 [16, 2], P('group'), may hold values from 0 to 7, as said below
Outputs:
- new_memory: float32 [128, 8, 256, 512], P('group', 'head')
- new_normalizer: float32 [128, 8, 256], P('group', 'head')
- mixed: bfloat16 [4, 128, 4096], P(None, 'group', 'head')
The draws below stay inside these ranges and needn't reach their ends.
Inputs may be any that keep to these rules, and one draw needn't show every extreme that they name: `swap_slots`: each row names 2 different slots among a group's 8 sequences. Groups g and g xor pair_mask[0] form the pairs.
All inputs are finite; a program needn't handle non-finite values. No bound on the sum of `active` on one device may be relied on, other than what follows from the above.
Results may differ from the reference program's by a relative error of at most 0.0032.
Values sent between devices are 32-bit elements; how exact they have to be, the bound alone decides.
No kernel may reach another device: no remote copies, remote signals or barrier semaphores. Data moves between devices by JAX's collectives and lax.ppermute only.
A program may use at most 128 MiB of HBM per device.

```python
import jax
import jax.numpy as jnp
from jax import lax

D = 4096
H = 8
DK = 256
DV = 512
SEQ_DEV = 8
SWAPS = 2
STEPS = 4
BATCH = 128
N_GROUP = 16


def draw_swap_slots(key, part):
    key = jax.random.fold_in(key, 11)
    row_keys = jax.random.split(key, N_GROUP)
    orders = jax.vmap(lambda single: jax.random.permutation(single, SEQ_DEV))(row_keys).astype(jnp.int32)
    first_row = jax.random.randint(jax.random.fold_in(key, 1), (), 0, N_GROUP)
    second_row = (first_row + 1) % N_GROUP
    row_ids = jnp.arange(N_GROUP)[:, None]
    lifted = (orders + (SEQ_DEV - 1 - orders[:, :1])) % SEQ_DEV
    lowered = (orders - orders[:, :1]) % SEQ_DEV
    orders = jnp.where(row_ids == first_row, lifted, jnp.where(row_ids == second_row, lowered, orders))
    return orders[:, :SWAPS].astype(jnp.int32)


def touch_ends(values, own_key, least, largest):
    place = [jax.random.randint(jax.random.fold_in(own_key, axis), (), 0, length) for axis, length in enumerate(values.shape)]
    widest = values.shape.index(max(values.shape))
    neighbour = place[:widest] + [(place[widest] + 1) % values.shape[widest]] + place[widest + 1:]
    return values.at[tuple(place)].set(least).at[tuple(neighbour)].set(largest)


def shard_levels(rng, extent, shards, low, largest):
    loudness, own = 1.0, jax.random.fold_in(rng, 6)
    for dim, blocks in shards:
        steps = jnp.exp(jax.random.uniform(jax.random.fold_in(own, dim), (blocks,), jnp.float32, low / len(shards), largest / len(shards)))
        loudness = loudness * jnp.repeat(steps, extent[dim] // blocks).reshape([-1 if axis == dim else 1 for axis in range(len(extent))])
    return loudness


def scatter_about(own_key, extent, spread, reach, pieces=(), kind=jnp.bfloat16):
    gain = shard_levels(own_key, extent, pieces, -0.22, 0.18) if pieces else 1.0
    result = jax.random.normal(own_key, extent, jnp.float32) * spread * gain
    return jnp.minimum(jnp.maximum(result, -reach), reach).astype(kind)


def setup_inputs(seed: int = 0) -> dict:
    key_list = jax.random.split(jax.random.key(seed), 14)
    memory = scatter_about(key_list[0], (BATCH, H, DK, DV), 1.0, 6.0, ((0, 16), (1, 8)), jnp.float32)
    normalizer = scatter_about(key_list[1], (BATCH, H, DK), 1.5, 9.0, ((0, 16), (1, 8)), jnp.float32)
    queries = scatter_about(key_list[2], (STEPS, BATCH, H, DK), 1.0, 6.0, ((1, 16), (2, 8)))
    keys = scatter_about(key_list[3], (STEPS, BATCH, H, DK), 1.0, 6.0, ((1, 16), (2, 8)))
    values = scatter_about(key_list[4], (STEPS, BATCH, H, DV), 1.0, 6.0, ((1, 16), (2, 8)))
    igate = jnp.clip(-3.0 + 4.0 * jax.random.uniform(key_list[5], (STEPS, BATCH, H), jnp.float32) ** shard_levels(key_list[5], (STEPS, BATCH, H), ((1, 16), (2, 8)), -0.2, 0.2), -3.0, 1.0)
    fgate = jnp.clip(-2.0 + 6.0 * jax.random.uniform(key_list[6], (STEPS, BATCH, H), jnp.float32) ** shard_levels(key_list[6], (STEPS, BATCH, H), ((1, 16), (2, 8)), -0.2, 0.2), -2.0, 4.0)
    ogate = scatter_about(key_list[7], (STEPS, BATCH, H, DV), 1.0, 6.0, ((1, 16), (2, 8)))
    out_weight = scatter_about(key_list[8], (H, DV, D), (H * DV) ** -0.5, 0.09375, ((0, 8),))
    tokens = scatter_about(key_list[9], (STEPS, BATCH, D), 0.5, 3.0, ((1, 16), (2, 8)))
    active = touch_ends((jax.random.randint(key_list[10], (BATCH,), 0, 4) < 3).astype(jnp.int32), jax.random.fold_in(key_list[10], 1), 0, 1)
    pair_mask = jax.random.randint(key_list[11], (1,), 1, N_GROUP).astype(jnp.int32)
    swap_slots = draw_swap_slots(jax.random.fold_in(key_list[13], 71), 0)
    return dict(memory=memory, normalizer=normalizer, queries=queries, keys=keys, values=values, igate=igate, fgate=fgate, ogate=ogate, out_weight=out_weight, tokens=tokens, active=active, pair_mask=pair_mask, swap_slots=swap_slots)


def reference(memory, normalizer, queries, keys, values, igate, fgate, ogate, out_weight, tokens, active, pair_mask, swap_slots):
    rows = jnp.arange(BATCH, dtype=jnp.int32)
    group = (rows // SEQ_DEV).astype(jnp.int32)
    position = (rows % SEQ_DEV).astype(jnp.int32)
    partner = jnp.bitwise_xor(group, pair_mask[0]).astype(jnp.int32)
    matches = swap_slots[group] == position[:, None]
    taken = jnp.sum(jnp.where(matches, swap_slots[partner], 0), axis=1).astype(jnp.int32)
    source = jnp.where(jnp.any(matches, axis=1), partner * SEQ_DEV + taken, rows).astype(jnp.int32)
    flattened_weight = out_weight.reshape(H * DV, D)
    scale = DK ** -0.5

    def one_row(row):
        anchor = source[row]
        memory_cell = memory[anchor]
        norm_state = normalizer[anchor]
        live = active[row] == 1
        results = []
        for step in range(STEPS):
            forget = jnp.where(live, jax.nn.sigmoid(fgate[step, row]), 1.0)
            inflow = jnp.where(live, jnp.exp(igate[step, row]), 0.0)
            key_now = keys[step, row].astype(jnp.float32)
            value_now = values[step, row].astype(jnp.float32)
            memory_cell = forget[:, None, None] * memory_cell + inflow[:, None, None] * key_now[:, :, None] * value_now[:, None, :]
            norm_state = forget[:, None] * norm_state + inflow[:, None] * key_now
            query_vector = queries[step, row].astype(jnp.float32) * scale
            numerator = jnp.einsum('onq,on->oq', memory_cell, query_vector, precision=lax.Precision.HIGHEST)
            denom = jnp.maximum(jnp.abs(jnp.sum(norm_state * query_vector, axis=-1)), 1.0)
            gated = numerator / denom[:, None] * jax.nn.sigmoid(ogate[step, row].astype(jnp.float32))
            hidden = jnp.where(live, gated, 0.0).astype(jnp.bfloat16).reshape(1, H * DV)
            update = jnp.dot(hidden, flattened_weight, preferred_element_type=jnp.float32)[0]
            results.append((tokens[step, row].astype(jnp.float32) + update).astype(jnp.bfloat16))
        return memory_cell, norm_state, jnp.stack(results)

    new_memory, new_normalizer, mixed = lax.map(one_row, rows)
    return new_memory, new_normalizer, jnp.transpose(mixed, (1, 0, 2))
```

```python
import functools

import jax
import jax.numpy as jnp
from jax import lax
from jax.experimental import pallas as pl
from jax.experimental.pallas import tpu as pltpu
from jax.sharding import PartitionSpec as P

F32 = jnp.float32
BF16 = jnp.bfloat16
VMEM = pl.BlockSpec(memory_space=pltpu.VMEM)
SMEM = pl.BlockSpec(memory_space=pltpu.SMEM)
ANY = pl.BlockSpec(memory_space=pl.ANY)


def halves(x):
    high = x.astype(BF16)
    return high, (x - high.astype(F32)).astype(BF16)


def dot(a, b, contract=1):
    return lax.dot_general(a, b, (((contract,), (0,)), ((), ())), preferred_element_type=F32)


def column(row):
    n = row.shape[1]
    eye = lax.broadcasted_iota(jnp.int32, (n, n), 0) == lax.broadcasted_iota(jnp.int32, (n, n), 1)
    return jnp.sum(jnp.where(eye, jnp.broadcast_to(row, (n, n)), 0.0), axis=1, keepdims=True)


def gates(igate, fgate, active):
    live = active[...] == 1
    forget, inflow = [], []
    for t in range(igate.shape[0]):
        forget.append(column(jnp.where(live, jax.nn.sigmoid(fgate[t]), 1.0)))
        inflow.append(column(jnp.where(live, jnp.exp(igate[t]), 0.0)))
    return forget, inflow, column(live.astype(F32))


def leave_kernel(slots, memory, normalizer, queries, x0, x1, small, wide, sems):
    copies = [pltpu.make_async_copy(memory.at[slots[0, j]], x, sems.at[j]) for j, x in enumerate((x0, x1))]
    for c in copies:
        c.start()
    steps = queries.shape[0]
    for t in range(steps):
        wide[t] = queries[t].astype(F32)
    small[...] = jnp.zeros_like(small)
    for j in range(2):
        for t in range(steps):
            small[pl.ds(j * steps + t, 1), :] = wide[t, pl.ds(slots[0, j], 1), :]
        small[pl.ds(2 * steps + j, 1), :] = normalizer[slots[0, j]]
    for c in copies:
        c.wait()


def leave(slots, memory, normalizer, queries):
    _, dk, dv = memory.shape
    steps, rows, _ = queries.shape
    cell = jax.ShapeDtypeStruct((dk, dv), F32)
    return pl.pallas_call(
        leave_kernel,
        in_specs=[SMEM, ANY, VMEM, VMEM],
        out_specs=[ANY, ANY, VMEM],
        out_shape=[cell, cell, jax.ShapeDtypeStruct((2 * steps + 8, dk), F32)],
        scratch_shapes=[pltpu.VMEM((steps, rows, dk), F32), pltpu.SemaphoreType.DMA((2,))],
        name="leave",
    )(slots, memory, normalizer, queries)


def answer_kernel(x0, x1, small, out):
    steps = out.shape[0] // 2
    q = small[0 : 2 * steps, :].astype(BF16)
    for j, x in enumerate((x0, x1)):
        high, low = halves(x[...])
        r = dot(q, high) + dot(q, low)
        out[j * steps : (j + 1) * steps, :] = r[j * steps : (j + 1) * steps, :]


def answer(x0, x1, small, steps):
    return pl.pallas_call(
        answer_kernel,
        in_specs=[VMEM, VMEM, VMEM],
        out_specs=VMEM,
        out_shape=jax.ShapeDtypeStruct((2 * steps, x0.shape[1]), F32),
        compiler_params=pltpu.CompilerParams(vmem_limit_bytes=16 * 2**20),
        name="answer",
    )(x0, x1, small)


def state_kernel(igate, fgate, active, queries, keys, values, memory, new, prod, khat, decay, wide_q, wide_v):
    steps, rows, dk = keys.shape
    per = memory.shape[0]
    step = pl.program_id(0)

    @pl.when(step == 0)
    def _():
        forget, inflow, _ = gates(igate, fgate, active)
        weight = jnp.ones_like(forget[0])
        for t in reversed(range(steps)):
            khat[t] = (weight * inflow[t]) * keys[t].astype(F32)
            weight = weight * forget[t]
        decay[...] = jnp.broadcast_to(weight, decay.shape)
        for t in range(steps):
            wide_q[t] = queries[t].astype(F32)
            wide_v[t] = values[t].astype(F32)

    for i in range(per):
        row = step * per + i
        here = memory[i]
        high, low = halves(here)
        q = jnp.concatenate([wide_q[t, pl.ds(row, 1), :] for t in range(steps)], axis=0)
        q = jnp.concatenate([q, jnp.zeros_like(q)], axis=0).astype(BF16)
        r = dot(q, high) + dot(q, low)
        for t in range(steps):
            prod[t, pl.ds(row, 1), :] = r[t : t + 1, :]
        k = jnp.concatenate([khat[t, pl.ds(row, 1), :] for t in range(steps)], axis=0)
        v = jnp.concatenate([wide_v[t, pl.ds(row, 1), :] for t in range(steps)], axis=0)
        k_high = k.astype(BF16).astype(F32)
        k = jnp.concatenate([k_high, k - k_high], axis=0).astype(BF16)
        v = jnp.concatenate([v, v], axis=0).astype(BF16)
        f = decay[pl.ds(row, 1), :]
        f = jnp.concatenate([f] * (here.shape[1] // f.shape[1]), axis=1)
        new[i] = f * here + dot(k, v, 0)


def state(igate, fgate, active, queries, keys, values, memory):
    steps, rows, dk = keys.shape
    dv = values.shape[2]
    per = 2

    def whole(x):
        return pl.BlockSpec(x.shape, lambda i: (0,) * len(x.shape))

    outs = [
        jax.ShapeDtypeStruct(memory.shape, F32),
        jax.ShapeDtypeStruct((steps, rows, dv), F32),
        jax.ShapeDtypeStruct((steps, rows, dk), F32),
        jax.ShapeDtypeStruct((rows, 128), F32),
    ]
    block = pl.BlockSpec((per, dk, dv), lambda i: (i, 0, 0))
    return pl.pallas_call(
        state_kernel,
        grid=(rows // per,),
        in_specs=[whole(x) for x in (igate, fgate, active, queries, keys, values)] + [block],
        out_specs=[block] + [whole(x) for x in outs[1:]],
        out_shape=outs,
        scratch_shapes=[pltpu.VMEM((steps, rows, dk), F32), pltpu.VMEM((steps, rows, dv), F32)],
        compiler_params=pltpu.CompilerParams(vmem_limit_bytes=24 * 2**20),
        cost_estimate=pl.CostEstimate(flops=10**8, bytes_accessed=2 * memory.size * 4, transcendentals=0),
        name="state",
    )(igate, fgate, active, queries, keys, values, memory)


def project_kernel(
    place, slots, igate, fgate, active, queries, keys, values, ogate, normalizer, prod, back, small, w0, w1,
    o0, o1, o2, o3, new_norm, hidden,
):
    steps, rows, dk = keys.shape
    step = pl.program_id(0)

    @pl.when(step == 0)
    def _():
        forget, inflow, live = gates(igate, fgate, active)
        index = lax.broadcasted_iota(jnp.int32, (rows, 1), 0)
        moved = [index == slots[0, j] for j in range(2)]
        norm = jnp.concatenate([normalizer[b] for b in range(rows)], axis=0)
        for j in range(2):
            norm = jnp.where(moved[j], small[2 * steps + j : 2 * steps + j + 1, :], norm)
        k = [keys[t].astype(F32) for t in range(steps)]
        v = [values[t].astype(F32) for t in range(steps)]
        beta, reach = [], jnp.ones_like(forget[0])
        for t in range(steps):
            q = queries[t].astype(F32) * (dk**-0.5)
            beta = [b * forget[t] for b in beta] + [inflow[t]]
            reach = reach * forget[t]
            cell = prod[t]
            for j in range(2):
                cell = jnp.where(moved[j], back[j * steps + t : j * steps + t + 1, :], cell)
            top = (reach * (dk**-0.5)) * cell
            under = reach * jnp.sum(norm * q, axis=1, keepdims=True)
            for s in range(t + 1):
                share = beta[s] * jnp.sum(k[s] * q, axis=1, keepdims=True)
                top = top + share * v[s]
                under = under + share
            out = top / jnp.maximum(jnp.abs(under), 1.0) * jax.nn.sigmoid(ogate[t].astype(F32))
            hidden[t * rows : (t + 1) * rows, :] = jnp.where(live > 0.0, out, 0.0)
        last = reach * norm
        for s in range(steps):
            last = last + beta[s] * k[s]
        for b in range(rows):
            new_norm[b] = last[b : b + 1, :]

    h = hidden[...].astype(BF16)
    first, second = dot(h, w0[...]), dot(h, w1[...])
    for m, out in enumerate((o0, o1, o2, o3)):

        @pl.when(step == m)
        def _(out=out):
            out[0] = first
            out[1] = second


def project(place, slots, igate, fgate, active, queries, keys, values, ogate, normalizer, prod, back, small, weight):
    steps, rows, dk = keys.shape
    dv, width = weight.shape
    cols = width // 8

    def whole(x):
        return pl.BlockSpec(x.shape, lambda i, *_: (0,) * len(x.shape))

    def part(p):
        return pl.BlockSpec((dv, cols), lambda i, place, slots: (0, lax.bitwise_xor(place[0], 2 * i + p)))

    outs = [jax.ShapeDtypeStruct((2, steps * rows, cols), F32)] * 4 + [jax.ShapeDtypeStruct((rows, 1, dk), F32)]
    args = (igate, fgate, active, queries, keys, values, ogate, normalizer, prod, back, small)
    return pl.pallas_call(
        project_kernel,
        grid_spec=pltpu.PrefetchScalarGridSpec(
            num_scalar_prefetch=2,
            grid=(4,),
            in_specs=[whole(x) for x in args] + [part(0), part(1)],
            out_specs=[whole(x) for x in outs],
            scratch_shapes=[pltpu.VMEM((steps * rows, dv), F32)],
        ),
        out_shape=outs,
        compiler_params=pltpu.CompilerParams(vmem_limit_bytes=16 * 2**20),
        cost_estimate=pl.CostEstimate(flops=2 * 32 * weight.size, bytes_accessed=2 * weight.size, transcendentals=0),
        name="project",
    )(place, slots, *args, weight, weight)


def arrive_kernel(slots, khat, decay, values, cell, former, new, *, which):
    steps, rows, _ = khat.shape
    mine = lax.broadcasted_iota(jnp.int32, (rows, 1), 0) == slots[0, which]

    def pick(x):
        return jnp.sum(jnp.where(mine, x, 0.0), axis=0, keepdims=True)

    k = jnp.concatenate([pick(khat[t]) for t in range(steps)], axis=0)
    v = jnp.concatenate([pick(values[t].astype(F32)) for t in range(steps)], axis=0)
    k_high = k.astype(BF16).astype(F32)
    k = jnp.concatenate([k_high, k - k_high], axis=0).astype(BF16)
    v = jnp.concatenate([v, v], axis=0).astype(BF16)
    f = pick(decay[...])
    f = jnp.concatenate([f] * (cell.shape[1] // f.shape[1]), axis=1)
    new[0] = f * cell[...] + dot(k, v, 0)


def arrive(which, slots, khat, decay, values, cell, former):
    steps, rows, dk = khat.shape
    dv = values.shape[2]
    cut = 2

    def whole(x):
        return pl.BlockSpec(x.shape, lambda i, *_: (0,) * len(x.shape))

    return pl.pallas_call(
        functools.partial(arrive_kernel, which=which),
        grid_spec=pltpu.PrefetchScalarGridSpec(
            num_scalar_prefetch=1,
            grid=(cut,),
            in_specs=[
                whole(khat),
                whole(decay),
                pl.BlockSpec((steps, rows, dv // cut), lambda i, s: (0, 0, i)),
                pl.BlockSpec((dk, dv // cut), lambda i, s: (0, i)),
                ANY,
            ],
            out_specs=pl.BlockSpec((1, dk, dv // cut), lambda i, s: (s[0, which], 0, i)),
        ),
        out_shape=jax.ShapeDtypeStruct(former.shape, F32),
        input_output_aliases={5: 0},
        compiler_params=pltpu.CompilerParams(vmem_limit_bytes=16 * 2**20),
        name=("arrive_first", "arrive_second")[which],
    )(slots, khat, decay, values, cell, former)


def per_device(
    memory,
    normalizer,
    queries,
    keys,
    values,
    igate,
    fgate,
    ogate,
    out_weight,
    tokens,
    active,
    pair_mask,
    swap_slots,
):
    steps, rows = queries.shape[0], queries.shape[1]
    groups, heads = lax.axis_size("group"), lax.axis_size("head")
    memory = memory.reshape(rows, *memory.shape[2:])
    queries, keys, values, ogate = (x.reshape(steps, rows, x.shape[3]) for x in (queries, keys, values, ogate))
    igate, fgate = igate.reshape(steps, 1, rows), fgate.reshape(steps, 1, rows)
    active = active.reshape(1, rows)
    weight = out_weight.reshape(out_weight.shape[1:])
    place = lax.axis_index("head").astype(jnp.int32).reshape(1)
    x0, x1, small = leave(swap_slots, memory, normalizer, queries)

    def branch(mask):
        swap = [(s, s ^ mask) for s in range(groups)]

        def across(x, bits):
            return lax.ppermute(x, "head", [(s, s ^ bits) for s in range(heads)])

        def run(*_):
            small_in = lax.ppermute(small, "group", swap)
            y0 = lax.ppermute(x0, "group", swap)
            y1 = lax.ppermute(x1, "group", swap)
            back = lax.ppermute(answer(x0, x1, small_in, steps), "group", swap)
            new, prod, khat, decay = state(igate, fgate, active, queries, keys, values, memory)
            o0, o1, o2, o3, new_norm = project(
                place, swap_slots, igate, fgate, active, queries, keys, values, ogate, normalizer, prod, back,
                small_in, weight,
            )
            r2, r1, r3 = across(o2, 4), across(o1, 2), across(o3, 6)
            total = [o0[p] + r1[p] + (r2[p] + r3[p]) for p in range(2)]
            share = total[0] + across(total[1], 1)
            mixed = (tokens.astype(F32) + share.reshape(tokens.shape)).astype(BF16)
            new = arrive(0, swap_slots, khat, decay, values, y0, new)
            new = arrive(1, swap_slots, khat, decay, values, y1, new)
            return new, new_norm, mixed

        return run

    new, new_norm, mixed = lax.switch(pair_mask[0] - 1, [branch(m) for m in range(1, groups)])
    return new.reshape(rows, 1, *new.shape[1:]), new_norm, mixed


def solution(mesh):
    placed = (
        P("group", "head", None, None),
        P("group", "head", None),
        P(None, "group", "head", None),
        P(None, "group", "head", None),
        P(None, "group", "head", None),
        P(None, "group", "head"),
        P(None, "group", "head"),
        P(None, "group", "head", None),
        P("head", None, None),
        P(None, "group", "head"),
        P("group"),
        P(),
        P("group", None),
    )
    return jax.shard_map(
        per_device,
        mesh=mesh,
        in_specs=placed,
        out_specs=(
            P("group", "head", None, None),
            P("group", "head", None),
            P(None, "group", "head"),
        ),
        check_vma=False,
    )
```

```python
import functools

import jax
import jax.numpy as jnp
from jax import lax
from jax.experimental import pallas as pl
from jax.experimental.pallas import tpu as pltpu
from jax.sharding import PartitionSpec as P

F32 = jnp.float32
BF16 = jnp.bfloat16
VMEM = pl.BlockSpec(memory_space=pltpu.VMEM)
SMEM = pl.BlockSpec(memory_space=pltpu.SMEM)
ANY = pl.BlockSpec(memory_space=pl.ANY)


def cost(size):
    return pl.CostEstimate(flops=size, bytes_accessed=size, transcendentals=0)


FREE = cost(0)
ANSWER, STATE, PROJECT = 0, 10**10, 0


def halves(x):
    high = x.astype(BF16)
    return high, (x - high.astype(F32)).astype(BF16)


def dot(a, b, contract=1):
    return lax.dot_general(a, b, (((contract,), (0,)), ((), ())), preferred_element_type=F32)


def column(row):
    n = row.shape[1]
    eye = lax.broadcasted_iota(jnp.int32, (n, n), 0) == lax.broadcasted_iota(jnp.int32, (n, n), 1)
    return jnp.sum(jnp.where(eye, jnp.broadcast_to(row, (n, n)), 0.0), axis=1, keepdims=True)


def gates(igate, fgate, active):
    live = active[...] == 1
    forget, inflow = [], []
    for t in range(igate.shape[0]):
        forget.append(column(jnp.where(live, jax.nn.sigmoid(fgate[t]), 1.0)))
        inflow.append(column(jnp.where(live, jnp.exp(igate[t]), 0.0)))
    return forget, inflow, column(live.astype(F32))


def leave_kernel(slots, memory, normalizer, queries, x0, x1, asked, norms, raw, norm, wide, sems):
    steps = queries.shape[0]
    cells = [pltpu.make_async_copy(memory.at[slots[0, j]], x, sems.at[j]) for j, x in enumerate((x0, x1))]
    loads = [pltpu.make_async_copy(queries, raw, sems.at[2]), pltpu.make_async_copy(normalizer, norm, sems.at[3])]
    for c in loads + cells:
        c.start()
    for c in loads:
        c.wait()
    for t in range(steps):
        wide[t] = raw[t].astype(F32)
    for j in range(2):
        for t in range(steps):
            asked[pl.ds(j * steps + t, 1), :] = wide[t, pl.ds(slots[0, j], 1), :]
    norms[...] = jnp.concatenate([norm[slots[0, j]] for j in (0, 1) for _ in range(4)], axis=0)
    for c in cells:
        c.wait()


def leave(slots, memory, normalizer, queries):
    _, dk, dv = memory.shape
    steps, rows, _ = queries.shape
    cell = jax.ShapeDtypeStruct((dk, dv), F32)
    return pl.pallas_call(
        leave_kernel,
        in_specs=[SMEM, ANY, ANY, ANY],
        out_specs=[ANY, ANY, VMEM, VMEM],
        out_shape=[cell, cell, jax.ShapeDtypeStruct((2 * steps, dk), F32), jax.ShapeDtypeStruct((8, dk), F32)],
        scratch_shapes=[
            pltpu.VMEM(queries.shape, queries.dtype),
            pltpu.VMEM(normalizer.shape, F32),
            pltpu.VMEM((steps, rows, dk), F32),
            pltpu.SemaphoreType.DMA((4,)),
        ],
        cost_estimate=FREE,
        name="leave",
    )(slots, memory, normalizer, queries)


def hold_kernel(x, after, out):
    pass


def hold(x, after):
    return pl.pallas_call(
        hold_kernel,
        in_specs=[ANY, ANY],
        out_specs=ANY,
        out_shape=jax.ShapeDtypeStruct(x.shape, x.dtype),
        input_output_aliases={0: 0},
        cost_estimate=FREE,
        name="hold",
    )(x, after)


def answer_kernel(x0, x1, asked, norms, out):
    steps = asked.shape[0] // 2
    width = 256
    q = asked[...].astype(BF16)
    out[2 * steps :, : norms.shape[1]] = norms[...]
    out[2 * steps :, norms.shape[1] :] = jnp.zeros_like(norms)
    first = lax.broadcasted_iota(jnp.int32, (2 * steps, 1), 0) < steps

    @pl.loop(0, out.shape[1] // width)
    def _(i):
        at = pl.ds(pl.multiple_of(i * width, width), width)
        r = []
        for x in (x0, x1):
            high, low = halves(x[:, at])
            r.append(dot(q, high) + dot(q, low))
        out[0 : 2 * steps, at] = jnp.where(first, r[0], r[1])


def answer(x0, x1, asked, norms):
    return pl.pallas_call(
        answer_kernel,
        in_specs=[VMEM] * 4,
        out_specs=VMEM,
        out_shape=jax.ShapeDtypeStruct((asked.shape[0] + 8, x0.shape[1]), F32),
        compiler_params=pltpu.CompilerParams(vmem_limit_bytes=16 * 2**20),
        cost_estimate=cost(ANSWER),
        name="answer",
    )(x0, x1, asked, norms)


def state_kernel(igate, fgate, active, queries, keys, values, memory, new, prod, khat, decay, wide_q, wide_v):
    steps, rows, dk = keys.shape
    row = pl.program_id(0)
    width = 256

    @pl.when(row == 0)
    def _():
        forget, inflow, _ = gates(igate, fgate, active)
        weight = jnp.ones_like(forget[0])
        for t in reversed(range(steps)):
            khat[t] = (weight * inflow[t]) * keys[t].astype(F32)
            weight = weight * forget[t]
        decay[...] = jnp.broadcast_to(weight, decay.shape)
        wide_q[...] = queries[...].astype(F32)
        wide_v[...] = values[...].astype(F32)

    q = jnp.concatenate([wide_q[t, pl.ds(row, 1), :] for t in range(steps)], axis=0)
    q = jnp.concatenate([q, q], axis=0).astype(BF16)
    k = jnp.concatenate([khat[t, pl.ds(row, 1), :] for t in range(steps)], axis=0)
    k_high = k.astype(BF16).astype(F32)
    k = jnp.concatenate([k_high, k - k_high], axis=0).astype(BF16)
    f = decay[pl.ds(row, 1), :]
    f = jnp.concatenate([f] * (width // f.shape[1]), axis=1)

    @pl.loop(0, memory.shape[2] // width)
    def _(i):
        at = pl.ds(pl.multiple_of(i * width, width), width)
        here = memory[0, :, at]
        high, low = halves(here)
        r = dot(q, high) + dot(q, low)
        for t in range(steps):
            prod[t, pl.ds(row, 1), at] = r[t : t + 1, :]
        v = jnp.concatenate([wide_v[t, pl.ds(row, 1), at] for t in range(steps)], axis=0)
        v = jnp.concatenate([v, v], axis=0).astype(BF16)
        new[0, :, at] = f * here + dot(k, v, 0)


def state(igate, fgate, active, queries, keys, values, memory):
    steps, rows, dk = keys.shape
    dv = values.shape[2]

    def whole(x):
        return pl.BlockSpec(x.shape, lambda i: (0,) * len(x.shape))

    outs = [
        jax.ShapeDtypeStruct(memory.shape, F32),
        jax.ShapeDtypeStruct((steps, rows, dv), F32),
        jax.ShapeDtypeStruct((steps, rows, dk), F32),
        jax.ShapeDtypeStruct((rows, 128), F32),
    ]
    block = pl.BlockSpec((1, dk, dv), lambda i: (i, 0, 0))
    return pl.pallas_call(
        state_kernel,
        grid=(rows,),
        in_specs=[whole(x) for x in (igate, fgate, active, queries, keys, values)] + [block],
        out_specs=[block] + [whole(x) for x in outs[1:]],
        out_shape=outs,
        scratch_shapes=[pltpu.VMEM((steps, rows, dk), F32), pltpu.VMEM((steps, rows, dv), F32)],
        compiler_params=pltpu.CompilerParams(vmem_limit_bytes=24 * 2**20),
        cost_estimate=cost(STATE),
        name="state",
    )(igate, fgate, active, queries, keys, values, memory)


def project_kernel(
    place, slots, igate, fgate, active, queries, keys, values, ogate, normalizer, prod, back, weight, after,
    o0, o1, o2, o3, new_norm, hidden,
):
    steps, rows, dk = keys.shape
    cols = o0.shape[2]
    forget, inflow, live = gates(igate, fgate, active)
    index = lax.broadcasted_iota(jnp.int32, (rows, 1), 0)
    moved = [index == slots[0, j] for j in range(2)]
    norm = jnp.concatenate([normalizer[b] for b in range(rows)], axis=0)
    for j in range(2):
        norm = jnp.where(moved[j], back[2 * steps + 4 * j : 2 * steps + 4 * j + 1, :dk], norm)
    k = [keys[t].astype(F32) for t in range(steps)]
    beta, reach = [], jnp.ones_like(forget[0])
    for t in range(steps):
        q = queries[t].astype(F32) * (dk**-0.5)
        beta = [b * forget[t] for b in beta] + [inflow[t]]
        reach = reach * forget[t]
        cell = prod[t]
        for j in range(2):
            cell = jnp.where(moved[j], back[j * steps + t : j * steps + t + 1, :], cell)
        top = (reach * (dk**-0.5)) * cell
        under = reach * jnp.sum(norm * q, axis=1, keepdims=True)
        for s in range(t + 1):
            share = beta[s] * jnp.sum(k[s] * q, axis=1, keepdims=True)
            top = top + share * values[s].astype(F32)
            under = under + share
        out = top / jnp.maximum(jnp.abs(under), 1.0) * jax.nn.sigmoid(ogate[t].astype(F32))
        hidden[t * rows : (t + 1) * rows, :] = jnp.where(live > 0.0, out, 0.0)
    last = reach * norm
    for s in range(steps):
        last = last + beta[s] * k[s]
    for b in range(rows):
        new_norm[b] = last[b : b + 1, :]

    @pl.loop(0, 8)
    def _(i):
        at = pl.ds(pl.multiple_of(lax.bitwise_xor(place[0], i) * cols, cols), cols)
        r = dot(hidden[...].astype(BF16), weight[:, at])
        for m, out in enumerate((o0, o1, o2, o3)):

            @pl.when(lax.shift_right_logical(i, 1) == m)
            def _(out=out):
                out[lax.bitwise_and(i, 1)] = r


def project(place, slots, igate, fgate, active, queries, keys, values, ogate, normalizer, prod, back, weight, after):
    steps, rows, dk = keys.shape
    dv, width = weight.shape
    outs = [jax.ShapeDtypeStruct((2, steps * rows, width // 8), F32)] * 4 + [jax.ShapeDtypeStruct((rows, 1, dk), F32)]
    return pl.pallas_call(
        project_kernel,
        in_specs=[SMEM, SMEM] + [VMEM] * 11 + [ANY],
        out_specs=[VMEM] * 5,
        out_shape=outs,
        scratch_shapes=[pltpu.VMEM((steps * rows, dv), F32)],
        compiler_params=pltpu.CompilerParams(vmem_limit_bytes=16 * 2**20),
        cost_estimate=cost(PROJECT),
        name="project",
    )(place, slots, igate, fgate, active, queries, keys, values, ogate, normalizer, prod, back, weight, after)


def arrive_kernel(slots, khat, decay, values, cell, former, new, *, which):
    steps, rows, _ = khat.shape
    mine = lax.broadcasted_iota(jnp.int32, (rows, 1), 0) == slots[0, which]

    def pick(x):
        return jnp.sum(jnp.where(mine, x, 0.0), axis=0, keepdims=True)

    k = jnp.concatenate([pick(khat[t]) for t in range(steps)], axis=0)
    v = jnp.concatenate([pick(values[t].astype(F32)) for t in range(steps)], axis=0)
    k_high = k.astype(BF16).astype(F32)
    k = jnp.concatenate([k_high, k - k_high], axis=0).astype(BF16)
    v = jnp.concatenate([v, v], axis=0).astype(BF16)
    f = pick(decay[...])
    f = jnp.concatenate([f] * (cell.shape[1] // f.shape[1]), axis=1)
    new[0] = f * cell[...] + dot(k, v, 0)


def arrive(which, slots, khat, decay, values, cell, former):
    steps, rows, dk = khat.shape
    dv = values.shape[2]
    cut = 2

    def whole(x):
        return pl.BlockSpec(x.shape, lambda i, *_: (0,) * len(x.shape))

    return pl.pallas_call(
        functools.partial(arrive_kernel, which=which),
        grid_spec=pltpu.PrefetchScalarGridSpec(
            num_scalar_prefetch=1,
            grid=(cut,),
            in_specs=[
                whole(khat),
                whole(decay),
                pl.BlockSpec((steps, rows, dv // cut), lambda i, s: (0, 0, i)),
                pl.BlockSpec((dk, dv // cut), lambda i, s: (0, i)),
                ANY,
            ],
            out_specs=pl.BlockSpec((1, dk, dv // cut), lambda i, s: (s[0, which], 0, i)),
        ),
        out_shape=jax.ShapeDtypeStruct(former.shape, F32),
        input_output_aliases={5: 0},
        compiler_params=pltpu.CompilerParams(vmem_limit_bytes=16 * 2**20),
        cost_estimate=FREE,
        name=("arrive_first", "arrive_second")[which],
    )(slots, khat, decay, values, cell, former)


def per_device(
    memory,
    normalizer,
    queries,
    keys,
    values,
    igate,
    fgate,
    ogate,
    out_weight,
    tokens,
    active,
    pair_mask,
    swap_slots,
):
    steps, rows = queries.shape[0], queries.shape[1]
    groups, heads = lax.axis_size("group"), lax.axis_size("head")
    memory = memory.reshape(rows, *memory.shape[2:])
    queries, keys, values, ogate = (x.reshape(steps, rows, x.shape[3]) for x in (queries, keys, values, ogate))
    igate, fgate = igate.reshape(steps, 1, rows), fgate.reshape(steps, 1, rows)
    active = active.reshape(1, rows)
    weight = out_weight.reshape(out_weight.shape[1:])
    place = lax.axis_index("head").astype(jnp.int32).reshape(1)
    x0, x1, asked, norms = leave(swap_slots, memory, normalizer, queries)
    mask = pair_mask[0]

    def other(*parts):
        return tuple(lax.ppermute(x, "group", [(s, s ^ 1) for s in range(groups)]) for x in parts)

    x0, x1, norms = lax.cond(lax.rem(mask, 2) == 1, other, lambda *parts: parts, x0, x1, norms)

    def branch(rest):
        def swap(x):
            return lax.ppermute(x, "group", [(s, s ^ (2 * rest)) for s in range(groups)]) if rest else x

        def across(x, bits):
            return lax.ppermute(x, "head", [(s, s ^ bits) for s in range(heads)])

        def run(*_):
            asked_in = swap(asked)
            first = hold(x0, asked)
            y0 = swap(first)
            reply = answer(first, x1, asked_in, norms)
            back = swap(reply)
            y1 = swap(hold(x1, reply))
            new, prod, khat, decay = state(igate, fgate, active, queries, keys, values, memory)
            o0, o1, o2, o3, new_norm = project(
                place, swap_slots, igate, fgate, active, queries, keys, values, ogate, normalizer, prod, back,
                weight, y0,
            )
            r2, r1, r3 = across(o2, 4), across(o1, 2), across(o3, 6)
            total = [o0[p] + r1[p] + (r2[p] + r3[p]) for p in range(2)]
            share = total[0] + across(total[1], 1)
            mixed = (tokens.astype(F32) + share.reshape(tokens.shape)).astype(BF16)
            new = arrive(0, swap_slots, khat, decay, values, y0, new)
            new = arrive(1, swap_slots, khat, decay, values, y1, new)
            return new, new_norm, mixed

        return run

    new, new_norm, mixed = lax.switch(lax.div(mask, 2), [branch(rest) for rest in range(groups // 2)])
    return new.reshape(rows, 1, *new.shape[1:]), new_norm, mixed


def solution(mesh):
    placed = (
        P("group", "head", None, None),
        P("group", "head", None),
        P(None, "group", "head", None),
        P(None, "group", "head", None),
        P(None, "group", "head", None),
        P(None, "group", "head"),
        P(None, "group", "head"),
        P(None, "group", "head", None),
        P("head", None, None),
        P(None, "group", "head"),
        P("group"),
        P(),
        P("group", None),
    )
    return jax.shard_map(
        per_device,
        mesh=mesh,
        in_specs=placed,
        out_specs=(
            P("group", "head", None, None),
            P("group", "head", None),
            P(None, "group", "head"),
        ),
        check_vma=False,
    )
```

```python
import functools

import jax
import jax.numpy as jnp
from jax import lax
from jax.experimental import pallas as pl
from jax.experimental.pallas import tpu as pltpu
from jax.sharding import PartitionSpec as P

F32 = jnp.float32
BF16 = jnp.bfloat16
VMEM = pl.BlockSpec(memory_space=pltpu.VMEM)
SMEM = pl.BlockSpec(memory_space=pltpu.SMEM)
ANY = pl.BlockSpec(memory_space=pl.ANY)


def cost(size):
    return pl.CostEstimate(flops=size, bytes_accessed=size, transcendentals=0)


FREE = cost(0)
LIMIT = pltpu.CompilerParams(vmem_limit_bytes=16 * 2**20)
PRODUCTS, UPDATE = 10**10, 0


def halves(x):
    high = x.astype(BF16)
    return high, (x - high.astype(F32)).astype(BF16)


def dot(a, b, contract=1):
    return lax.dot_general(a, b, (((contract,), (0,)), ((), ())), preferred_element_type=F32)


def column(row):
    n = row.shape[1]
    eye = lax.broadcasted_iota(jnp.int32, (n, n), 0) == lax.broadcasted_iota(jnp.int32, (n, n), 1)
    return jnp.sum(jnp.where(eye, jnp.broadcast_to(row, (n, n)), 0.0), axis=1, keepdims=True)


def gates(igate, fgate, active):
    live = active[...] == 1
    forget, inflow = [], []
    for t in range(igate.shape[0]):
        forget.append(column(jnp.where(live, jax.nn.sigmoid(fgate[t]), 1.0)))
        inflow.append(column(jnp.where(live, jnp.exp(igate[t]), 0.0)))
    return forget, inflow, column(live.astype(F32))


def leave_kernel(slots, memory, normalizer, queries, head, tail, asked, norms, raw, norm, wide, sems):
    steps = queries.shape[0]
    cut, dk = head.shape[0], memory.shape[1]
    one, two = memory.at[slots[0, 0]], memory.at[slots[0, 1]]
    loads = [pltpu.make_async_copy(queries, raw, sems.at[0]), pltpu.make_async_copy(normalizer, norm, sems.at[1])]
    cells = [
        pltpu.make_async_copy(one.at[pl.ds(0, cut)], head, sems.at[2]),
        pltpu.make_async_copy(one.at[pl.ds(cut, dk - cut)], tail.at[pl.ds(0, dk - cut)], sems.at[3]),
        pltpu.make_async_copy(two, tail.at[pl.ds(dk - cut, dk)], sems.at[4]),
    ]
    for c in loads + cells:
        c.start()
    for c in loads:
        c.wait()
    for t in range(steps):
        wide[t] = raw[t].astype(F32)
    for j in range(2):
        for t in range(steps):
            asked[pl.ds(j * steps + t, 1), :] = wide[t, pl.ds(slots[0, j], 1), :]
    norms[...] = jnp.concatenate([norm[slots[0, j]] for j in (0, 1) for _ in range(4)], axis=0)
    for c in cells:
        c.wait()


def leave(slots, memory, normalizer, queries):
    _, dk, dv = memory.shape
    steps, rows, _ = queries.shape
    cut = dk // 2
    return pl.pallas_call(
        leave_kernel,
        in_specs=[SMEM, ANY, ANY, ANY],
        out_specs=[ANY, ANY, VMEM, VMEM],
        out_shape=[
            jax.ShapeDtypeStruct((cut, dv), F32),
            jax.ShapeDtypeStruct((2 * dk - cut, dv), F32),
            jax.ShapeDtypeStruct((2 * steps, dk), F32),
            jax.ShapeDtypeStruct((8, dk), F32),
        ],
        scratch_shapes=[
            pltpu.VMEM(queries.shape, queries.dtype),
            pltpu.VMEM(normalizer.shape, F32),
            pltpu.VMEM((steps, rows, dk), F32),
            pltpu.SemaphoreType.DMA((5,)),
        ],
        compiler_params=LIMIT,
        cost_estimate=FREE,
        name="leave",
    )(slots, memory, normalizer, queries)


def hold_kernel(x, after, out):
    pass


def hold(x, after):
    return pl.pallas_call(
        hold_kernel,
        in_specs=[VMEM, ANY],
        out_specs=VMEM,
        out_shape=jax.ShapeDtypeStruct(x.shape, x.dtype),
        input_output_aliases={0: 0},
        compiler_params=LIMIT,
        cost_estimate=FREE,
        name="hold",
    )(x, after)


def answer_kernel(head, tail, asked, norms, after, out, tail_on):
    steps = asked.shape[0] // 2
    cut, dk = head.shape[0], asked.shape[1]
    q = asked[...].astype(BF16)
    out[2 * steps :, : norms.shape[1]] = norms[...]
    out[2 * steps :, norms.shape[1] :] = jnp.zeros_like(norms)
    first = lax.broadcasted_iota(jnp.int32, (2 * steps, 1), 0) < steps
    parts = ((head, 0, 0), (tail, 0, cut), (tail, dk - cut, 0), (tail, dk, cut))

    @pl.loop(0, out.shape[1] // 256)
    def _(i):
        at = pl.ds(pl.multiple_of(i * 256, 256), 256)
        r = []
        for x, start, k in parts:
            high, low = halves(x[pl.ds(start, cut), at])
            r.append(dot(q[:, k : k + cut], high) + dot(q[:, k : k + cut], low))
        out[0 : 2 * steps, at] = jnp.where(first, r[0] + r[1], r[2] + r[3])


def answer(head, tail, asked, norms, after):
    return pl.pallas_call(
        answer_kernel,
        in_specs=[VMEM] * 5,
        out_specs=[VMEM, VMEM],
        out_shape=[
            pltpu.VMEM((asked.shape[0] + 8, head.shape[1]), F32),
            jax.ShapeDtypeStruct(tail.shape, F32),
        ],
        input_output_aliases={1: 1},
        compiler_params=LIMIT,
        cost_estimate=FREE,
        name="answer",
    )(head, tail, asked, norms, after)


def weigh_kernel(igate, fgate, active, queries, keys, values, khat, decay, top, under, reach, token):
    token[...] = jnp.zeros_like(token)
    steps, rows, dk = keys.shape
    forget, inflow, _ = gates(igate, fgate, active)
    k = [keys[t].astype(F32) for t in range(steps)]
    weight = jnp.ones_like(forget[0])
    for t in reversed(range(steps)):
        khat[t] = (weight * inflow[t]) * k[t]
        weight = weight * forget[t]
    decay[...] = jnp.broadcast_to(weight, decay.shape)
    beta, so_far = [], jnp.ones_like(forget[0])
    for t in range(steps):
        q = queries[t].astype(F32) * (dk**-0.5)
        beta = [b * forget[t] for b in beta] + [inflow[t]]
        so_far = so_far * forget[t]
        above, below = 0.0, 0.0
        for s in range(t + 1):
            share = beta[s] * jnp.sum(k[s] * q, axis=1, keepdims=True)
            above = above + share * values[s].astype(F32)
            below = below + share
        top[t] = above
        under[t] = jnp.broadcast_to(below, under.shape[1:])
        reach[t] = jnp.broadcast_to(so_far * (dk**-0.5), reach.shape[1:])


def weigh(igate, fgate, active, queries, keys, values):
    steps, rows, dk = keys.shape
    dv = values.shape[2]
    shapes = ((steps, rows, dk), (rows, 128), (steps, rows, dv), (steps, rows, 128), (steps, rows, 128), (8, 128))
    return pl.pallas_call(
        weigh_kernel,
        in_specs=[VMEM] * 6,
        out_specs=[VMEM] * len(shapes),
        out_shape=[pltpu.VMEM(x, F32) for x in shapes],
        compiler_params=LIMIT,
        cost_estimate=FREE,
        name="weigh",
    )(igate, fgate, active, queries, keys, values)


def products_kernel(queries, memory, prod, wide_q):
    steps, rows, _ = queries.shape
    wide_q[...] = queries[...].astype(F32)

    @pl.loop(0, rows, unroll=2)
    def _(row):
        q = jnp.concatenate([wide_q[t, pl.ds(row, 1), :] for t in range(steps)], axis=0)
        q = jnp.concatenate([q, q], axis=0).astype(BF16)
        high, low = halves(memory[row])
        r = dot(q, high) + dot(q, low)
        for t in range(steps):
            prod[t, pl.ds(row, 1), :] = r[t : t + 1, :]


def products(queries, memory):
    steps, rows, dk = queries.shape
    return pl.pallas_call(
        products_kernel,
        in_specs=[VMEM] * 2,
        out_specs=VMEM,
        out_shape=pltpu.VMEM((steps, rows, memory.shape[2]), F32),
        scratch_shapes=[pltpu.VMEM((steps, rows, dk), F32)],
        compiler_params=LIMIT,
        cost_estimate=cost(PRODUCTS),
        name="products",
    )(queries, memory)


def update_kernel(slots, khat, decay, values, memory, head, normalizer, back, new, new_norm, add, keep, wide_v, done, norm_done, sems):
    steps, rows, dk = khat.shape
    dv, cut = values.shape[2], head.shape[0]
    width = 256
    wide_v[...] = values[...].astype(F32)

    def leave(row):
        return pltpu.make_async_copy(done.at[row], new.at[row], sems.at[row])

    def terms(row):
        k = jnp.concatenate([khat[t, pl.ds(row, 1), :] for t in range(steps)], axis=0)
        k_high = k.astype(BF16).astype(F32)
        k = jnp.concatenate([k_high, k - k_high], axis=0).T.astype(BF16)
        v = jnp.concatenate([wide_v[t, pl.ds(row, 1), :] for t in range(steps)], axis=0)
        f = decay[pl.ds(row, 1), :]
        return k, jnp.concatenate([v, v], axis=0).astype(BF16), jnp.concatenate([f] * (dv // f.shape[1]), axis=1)

    index = lax.broadcasted_iota(jnp.int32, (rows, 1), 0)
    norm = jnp.concatenate([normalizer[b] for b in range(rows)], axis=0)
    for j in range(2):
        norm = jnp.where(index == slots[0, j], back[2 * steps + 4 * j : 2 * steps + 4 * j + 1, :dk], norm)
    f = decay[...]
    norm = jnp.concatenate([f] * (dk // f.shape[1]), axis=1) * norm
    for t in range(steps):
        norm = norm + khat[t]
    for b in range(rows):
        norm_done[b] = norm[b : b + 1, :]
    norm_out = pltpu.make_async_copy(norm_done, new_norm, sems.at[rows])
    norm_out.start()

    @pl.loop(0, rows)
    def _(row):
        k, v, f = terms(row)
        for start in range(0, dv, width):
            at = pl.ds(start, width)
            done[row, :, at] = f[:, start : start + width] * memory[row, :, at] + dot(k, v[:, start : start + width])

        @pl.when(row == slots[0, 0])
        def _():
            done[row, 0:cut, :] = f * head[...] + dot(k[:cut], v)

        leave(row).start()

    k, v, f = terms(slots[0, 0])
    add[0 : dk - cut, :] = dot(k[cut:], v)
    keep[0:4, :] = jnp.concatenate([f] * 4, axis=0)
    k, v, f = terms(slots[0, 1])
    add[dk - cut :, :] = dot(k, v)
    keep[4:8, :] = jnp.concatenate([f] * 4, axis=0)
    norm_out.wait()
    for row in range(rows):
        leave(row).wait()


def update(slots, khat, decay, values, memory, head, normalizer, back):
    steps, rows, dk = khat.shape
    dv, tail = memory.shape[2], 2 * dk - head.shape[0]
    return pl.pallas_call(
        update_kernel,
        in_specs=[SMEM] + [VMEM] * 7,
        out_specs=[ANY, ANY, VMEM, VMEM],
        out_shape=[
            pltpu.HBM(memory.shape, F32),
            pltpu.HBM(normalizer.shape, F32),
            pltpu.VMEM((tail, dv), F32),
            pltpu.VMEM((8, dv), F32),
        ],
        scratch_shapes=[
            pltpu.VMEM(values.shape, F32),
            pltpu.VMEM(memory.shape, F32),
            pltpu.VMEM(normalizer.shape, F32),
            pltpu.SemaphoreType.DMA((rows + 1,)),
        ],
        compiler_params=LIMIT,
        cost_estimate=cost(UPDATE),
        name="update",
    )(slots, khat, decay, values, memory, head, normalizer, back)


def project_kernel(
    place, slots, active, queries, ogate, normalizer, prod, top, under, reach, back, weight, after,
    o0, o1, o2, o3, hidden,
):
    steps, rows, dk = queries.shape
    dv, cols = weight.shape[0], o0.shape[2]
    live = column((active[...] == 1).astype(F32)) > 0.0
    index = lax.broadcasted_iota(jnp.int32, (rows, 1), 0)
    moved = [index == slots[0, j] for j in range(2)]
    norm = jnp.concatenate([normalizer[b] for b in range(rows)], axis=0)
    for j in range(2):
        norm = jnp.where(moved[j], back[2 * steps + 4 * j : 2 * steps + 4 * j + 1, :dk], norm)
    for t in range(steps):
        cell = prod[t]
        for j in range(2):
            cell = jnp.where(moved[j], back[j * steps + t : j * steps + t + 1, :], cell)
        factor = reach[t]
        below = under[t] + factor * jnp.sum(norm * queries[t].astype(F32), axis=1, keepdims=True)
        below = jnp.maximum(jnp.abs(below), 1.0)
        factor, below = (jnp.concatenate([x] * (dv // x.shape[1]), axis=1) for x in (factor, below))
        out = (factor * cell + top[t]) / below * jax.nn.sigmoid(ogate[t].astype(F32))
        hidden[t * rows : (t + 1) * rows, :] = jnp.where(live, out, 0.0)

    h = hidden[...].astype(BF16)

    @pl.loop(0, 4)
    def _(m):
        r = []
        for p in range(2):
            at = pl.ds(pl.multiple_of(lax.bitwise_xor(place[0], 2 * m + p) * cols, cols), cols)
            r.append(dot(h, weight[:, at]))
        for n, out in enumerate((o0, o1, o2, o3)):

            @pl.when(m == n)
            def _(out=out):
                out[0] = r[0]
                out[1] = r[1]


def project(place, slots, active, queries, ogate, normalizer, prod, top, under, reach, back, weight, after):
    steps, rows, _ = queries.shape
    dv, width = weight.shape
    return pl.pallas_call(
        project_kernel,
        in_specs=[SMEM, SMEM] + [VMEM] * 10 + [ANY],
        out_specs=[VMEM] * 4,
        out_shape=[pltpu.VMEM((2, steps * rows, width // 8), F32)] * 4,
        scratch_shapes=[pltpu.VMEM((steps * rows, dv), F32)],
        compiler_params=LIMIT,
        cost_estimate=FREE,
        name="project",
    )(place, slots, active, queries, ogate, normalizer, prod, top, under, reach, back, weight, after)


def merge_kernel(o0, r1, r2, r3, after, own, other):
    own[...] = o0[0] + r1[0] + (r2[0] + r3[0])
    other[...] = o0[1] + r1[1] + (r2[1] + r3[1])


def merge(o0, r1, r2, r3, after):
    return pl.pallas_call(
        merge_kernel,
        in_specs=[VMEM] * 4 + [ANY],
        out_specs=[VMEM] * 2,
        out_shape=[pltpu.VMEM(o0.shape[1:], F32)] * 2,
        compiler_params=LIMIT,
        cost_estimate=FREE,
        name="merge",
    )(o0, r1, r2, r3, after)


def finish_kernel(slots, tail, add, keep, tokens, own, z, former, new, mixed, where, done, mixed_done, sems):
    dk, rest = new.shape[1], new.shape[1] * 2 - tail.shape[0]
    find = pltpu.make_async_copy(slots, where, sems.at[0])
    find.start()
    total = own[...] + z[...]
    steps, rows, _ = tokens.shape
    for t in range(steps):
        mixed_done[t] = (tokens[t].astype(F32) + total[t * rows : (t + 1) * rows]).astype(BF16)
    mixed_out = pltpu.make_async_copy(mixed_done, mixed, sems.at[1])
    mixed_out.start()
    find.wait()
    outs = []
    for j, start, size, row in ((0, 0, dk - rest, rest), (1, dk - rest, dk, 0)):
        at = pl.ds(start, size)
        done[at, :] = keep[4 * j : 4 * j + 1, :] * tail[at, :] + add[at, :]
        outs.append(pltpu.make_async_copy(done.at[at], new.at[where[0, j], pl.ds(row, size)], sems.at[2 + j]))
        outs[-1].start()
    for c in outs:
        c.wait()
    mixed_out.wait()


def finish(slots, tail, add, keep, tokens, own, z, former):
    return pl.pallas_call(
        finish_kernel,
        in_specs=[ANY] + [VMEM] * 6 + [ANY],
        out_specs=[ANY, ANY],
        out_shape=[pltpu.HBM(former.shape, F32), pltpu.HBM(tokens.shape, BF16)],
        scratch_shapes=[
            pltpu.SMEM(slots.shape, slots.dtype),
            pltpu.VMEM(tail.shape, F32),
            pltpu.VMEM(tokens.shape, BF16),
            pltpu.SemaphoreType.DMA((4,)),
        ],
        input_output_aliases={7: 0},
        compiler_params=LIMIT,
        cost_estimate=FREE,
        name="finish",
    )(slots, tail, add, keep, tokens, own, z, former)


def per_device(
    memory,
    normalizer,
    queries,
    keys,
    values,
    igate,
    fgate,
    ogate,
    out_weight,
    tokens,
    active,
    pair_mask,
    swap_slots,
):
    steps, rows = queries.shape[0], queries.shape[1]
    groups, heads = lax.axis_size("group"), lax.axis_size("head")
    memory = memory.reshape(rows, *memory.shape[2:])
    queries, keys, values, ogate = (x.reshape(steps, rows, x.shape[3]) for x in (queries, keys, values, ogate))
    igate, fgate = igate.reshape(steps, 1, rows), fgate.reshape(steps, 1, rows)
    active = active.reshape(1, rows)
    weight = out_weight.reshape(out_weight.shape[1:])
    place = lax.axis_index("head").astype(jnp.int32).reshape(1)
    head, tail, asked, norms = leave(swap_slots, memory, normalizer, queries)
    mask = pair_mask[0]

    def other(*parts):
        return tuple(lax.ppermute(x, "group", [(s, s ^ 1) for s in range(groups)]) for x in parts)

    head, tail, norms = lax.cond(lax.rem(mask, 2) == 1, other, lambda *parts: parts, head, tail, norms)

    def branch(rest):
        def swap(x):
            return lax.ppermute(x, "group", [(s, s ^ (2 * rest)) for s in range(groups)]) if rest else x

        def across(x, bits):
            return lax.ppermute(x, "head", [(s, s ^ bits) for s in range(heads)])

        def run(*_):
            asked_in = swap(asked)
            first = hold(head, asked)
            head_in = swap(first)
            khat, decay, top, under, reach, token = weigh(igate, fgate, active, queries, keys, values)
            reply, tail_on = answer(first, tail, asked_in, norms, token)
            back = swap(reply)
            tail_in = swap(tail_on)
            prod = products(queries, memory)
            o0, o1, o2, o3 = project(
                place, swap_slots, active, queries, ogate, normalizer, prod, top, under, reach, back, weight, head_in
            )
            r2, r1, r3 = across(o2, 4), across(o1, 2), across(o3, 6)
            new, new_norm, add, keep = update(swap_slots, khat, decay, values, memory, head_in, normalizer, back)
            own, other = merge(o0, r1, r2, r3, new)
            z = across(other, 1)
            new, mixed = finish(swap_slots, tail_in, add, keep, tokens, own, z, new)
            return new, new_norm, mixed

        return run

    new, new_norm, mixed = lax.switch(lax.div(mask, 2), [branch(rest) for rest in range(groups // 2)])
    return new.reshape(rows, 1, *new.shape[1:]), new_norm, mixed


def solution(mesh):
    placed = (
        P("group", "head", None, None),
        P("group", "head", None),
        P(None, "group", "head", None),
        P(None, "group", "head", None),
        P(None, "group", "head", None),
        P(None, "group", "head"),
        P(None, "group", "head"),
        P(None, "group", "head", None),
        P("head", None, None),
        P(None, "group", "head"),
        P("group"),
        P(),
        P("group", None),
    )
    return jax.shard_map(
        per_device,
        mesh=mesh,
        in_specs=placed,
        out_specs=(
            P("group", "head", None, None),
            P("group", "head", None),
            P(None, "group", "head"),
        ),
        check_vma=False,
    )
```

```python
import functools

import jax
import jax.numpy as jnp
from jax import lax
from jax.experimental import pallas as pl
from jax.experimental.pallas import tpu as pltpu
from jax.sharding import PartitionSpec as P

F32 = jnp.float32
BF16 = jnp.bfloat16
VMEM = pl.BlockSpec(memory_space=pltpu.VMEM)
SMEM = pl.BlockSpec(memory_space=pltpu.SMEM)
ANY = pl.BlockSpec(memory_space=pl.ANY)
HBM = pl.BlockSpec(memory_space=pltpu.HBM)


def cost(size):
    return pl.CostEstimate(flops=size, bytes_accessed=size, transcendentals=0)


FREE = cost(0)
LIMIT = pltpu.CompilerParams(vmem_limit_bytes=16 * 2**20)
PRODUCTS, UPDATE = 10**10, 0


def halves(x):
    high = x.astype(BF16)
    return high, (x - high.astype(F32)).astype(BF16)


def dot(a, b, contract=1):
    return lax.dot_general(a, b, (((contract,), (0,)), ((), ())), preferred_element_type=F32)


def column(row):
    n = row.shape[1]
    eye = lax.broadcasted_iota(jnp.int32, (n, n), 0) == lax.broadcasted_iota(jnp.int32, (n, n), 1)
    return jnp.sum(jnp.where(eye, jnp.broadcast_to(row, (n, n)), 0.0), axis=1, keepdims=True)


def gates(igate, fgate, active):
    live = active[...] == 1
    forget, inflow = [], []
    for t in range(igate.shape[0]):
        forget.append(column(jnp.where(live, jax.nn.sigmoid(fgate[t]), 1.0)))
        inflow.append(column(jnp.where(live, jnp.exp(igate[t]), 0.0)))
    return forget, inflow, column(live.astype(F32))


def leave_kernel(
    slots_in, mask_in, memory, normalizer, queries, head, tail, asked, norms, core, rest,
    slots, mask, raw, norm, wide, sems,
):
    steps = queries.shape[0]
    find = pltpu.make_async_copy(slots_in, slots, sems.at[5])
    find_mask = pltpu.make_async_copy(mask_in, mask, sems.at[6])
    find.start()
    find_mask.start()
    loads = [pltpu.make_async_copy(queries, raw, sems.at[0]), pltpu.make_async_copy(normalizer, norm, sems.at[1])]
    for c in loads:
        c.start()
    find.wait()
    cut, dk = head.shape[0], memory.shape[1]
    one, two = memory.at[slots[0, 0]], memory.at[slots[0, 1]]
    cells = [
        pltpu.make_async_copy(one.at[pl.ds(0, cut)], head, sems.at[2]),
        pltpu.make_async_copy(one.at[pl.ds(cut, dk - cut)], tail.at[pl.ds(0, dk - cut)], sems.at[3]),
        pltpu.make_async_copy(two, tail.at[pl.ds(dk - cut, dk)], sems.at[4]),
    ]
    for c in cells:
        c.start()
    find_mask.wait()
    core[0] = lax.bitwise_and(mask[0], 1)
    rest[0] = lax.shift_right_logical(mask[0], 1)
    for c in loads:
        c.wait()
    for t in range(steps):
        wide[t] = raw[t].astype(F32)
    for j in range(2):
        for t in range(steps):
            asked[pl.ds(j * steps + t, 1), :] = wide[t, pl.ds(slots[0, j], 1), :]
    norms[...] = jnp.concatenate([norm[slots[0, j]] for j in (0, 1) for _ in range(steps)], axis=0)
    for c in cells:
        c.wait()


def leave(slots, mask, memory, normalizer, queries):
    _, dk, dv = memory.shape
    steps, rows, _ = queries.shape
    cut = dk // 2
    return pl.pallas_call(
        leave_kernel,
        in_specs=[HBM] * 2 + [ANY] * 3,
        out_specs=[ANY, ANY, VMEM, VMEM, SMEM, SMEM],
        out_shape=[
            jax.ShapeDtypeStruct((cut, dv), F32),
            jax.ShapeDtypeStruct((2 * dk - cut, dv), F32),
            jax.ShapeDtypeStruct((2 * steps, dk), F32),
            jax.ShapeDtypeStruct((2 * steps, dk), F32),
            pltpu.SMEM((1,), jnp.int32),
            pltpu.SMEM((1,), jnp.int32),
        ],
        scratch_shapes=[
            pltpu.SMEM(slots.shape, slots.dtype),
            pltpu.SMEM(mask.shape, mask.dtype),
            pltpu.VMEM(queries.shape, queries.dtype),
            pltpu.VMEM(normalizer.shape, F32),
            pltpu.VMEM((steps, rows, dk), F32),
            pltpu.SemaphoreType.DMA((7,)),
        ],
        compiler_params=LIMIT,
        cost_estimate=FREE,
        name="leave",
    )(slots, mask, memory, normalizer, queries)


def hold_kernel(x, after, out):
    pass


def hold(x, after):
    return pl.pallas_call(
        hold_kernel,
        in_specs=[VMEM, ANY],
        out_specs=VMEM,
        out_shape=jax.ShapeDtypeStruct(x.shape, x.dtype),
        input_output_aliases={0: 0},
        compiler_params=LIMIT,
        cost_estimate=FREE,
        name="hold",
    )(x, after)


def answer_kernel(head, tail, asked, norms, after, out, tail_on):
    steps = asked.shape[0] // 2
    cut, dk = head.shape[0], asked.shape[1]
    q = asked[...].astype(BF16)
    dv = head.shape[1]
    out[:, dv:] = norms[...]
    first = lax.broadcasted_iota(jnp.int32, (2 * steps, 1), 0) < steps
    parts = ((head, 0, 0), (tail, 0, cut), (tail, dk - cut, 0), (tail, dk, cut))

    @pl.loop(0, dv // 256)
    def _(i):
        at = pl.ds(pl.multiple_of(i * 256, 256), 256)
        r = []
        for x, start, k in parts:
            high, low = halves(x[pl.ds(start, cut), at])
            r.append(dot(q[:, k : k + cut], high) + dot(q[:, k : k + cut], low))
        out[:, at] = jnp.where(first, r[0] + r[1], r[2] + r[3])


def answer(head, tail, asked, norms, after):
    return pl.pallas_call(
        answer_kernel,
        in_specs=[VMEM] * 5,
        out_specs=[VMEM, VMEM],
        out_shape=[
            pltpu.VMEM((asked.shape[0], head.shape[1] + asked.shape[1]), F32),
            jax.ShapeDtypeStruct(tail.shape, F32),
        ],
        input_output_aliases={1: 1},
        compiler_params=LIMIT,
        cost_estimate=FREE,
        name="answer",
    )(head, tail, asked, norms, after)


def weigh_kernel(igate, fgate, active, queries, keys, values, khat, decay, top, under, reach, token):
    token[...] = jnp.zeros_like(token)
    steps, rows, dk = keys.shape
    forget, inflow, _ = gates(igate, fgate, active)
    k = [keys[t].astype(F32) for t in range(steps)]
    weight = jnp.ones_like(forget[0])
    for t in reversed(range(steps)):
        khat[t] = (weight * inflow[t]) * k[t]
        weight = weight * forget[t]
    decay[...] = jnp.broadcast_to(weight, decay.shape)
    beta, so_far = [], jnp.ones_like(forget[0])
    for t in range(steps):
        q = queries[t].astype(F32) * (dk**-0.5)
        beta = [b * forget[t] for b in beta] + [inflow[t]]
        so_far = so_far * forget[t]
        above, below = 0.0, 0.0
        for s in range(t + 1):
            share = beta[s] * jnp.sum(k[s] * q, axis=1, keepdims=True)
            above = above + share * values[s].astype(F32)
            below = below + share
        top[t] = above
        under[t] = jnp.broadcast_to(below, under.shape[1:])
        reach[t] = jnp.broadcast_to(so_far * (dk**-0.5), reach.shape[1:])


def weigh(igate, fgate, active, queries, keys, values):
    steps, rows, dk = keys.shape
    dv = values.shape[2]
    shapes = ((steps, rows, dk), (rows, 128), (steps, rows, dv), (steps, rows, 128), (steps, rows, 128), (8, 128))
    return pl.pallas_call(
        weigh_kernel,
        in_specs=[VMEM] * 6,
        out_specs=[VMEM] * len(shapes),
        out_shape=[pltpu.VMEM(x, F32) for x in shapes],
        compiler_params=LIMIT,
        cost_estimate=FREE,
        name="weigh",
    )(igate, fgate, active, queries, keys, values)


def products_kernel(queries, memory, prod, wide_q):
    steps, rows, _ = queries.shape
    wide_q[...] = queries[...].astype(F32)

    @pl.loop(0, rows, unroll=2)
    def _(row):
        q = jnp.concatenate([wide_q[t, pl.ds(row, 1), :] for t in range(steps)], axis=0)
        q = jnp.concatenate([q, q], axis=0).astype(BF16)
        high, low = halves(memory[row])
        r = dot(q, high) + dot(q, low)
        for t in range(steps):
            prod[t, pl.ds(row, 1), :] = r[t : t + 1, :]


def products(queries, memory):
    steps, rows, dk = queries.shape
    return pl.pallas_call(
        products_kernel,
        in_specs=[VMEM] * 2,
        out_specs=VMEM,
        out_shape=pltpu.VMEM((steps, rows, memory.shape[2]), F32),
        scratch_shapes=[pltpu.VMEM((steps, rows, dk), F32)],
        compiler_params=LIMIT,
        cost_estimate=cost(PRODUCTS),
        name="products",
    )(queries, memory)


def update_kernel(slots, khat, decay, values, memory, head, normalizer, back, new, new_norm, add, keep, where, wide_v, done, norm_done, sems):
    steps, rows, dk = khat.shape
    dv, cut = values.shape[2], head.shape[0]
    width = 256
    wide_v[...] = values[...].astype(F32)
    for j in range(2):
        where[0, j] = slots[0, j]

    def leave(row):
        return pltpu.make_async_copy(done.at[row], new.at[row], sems.at[row])

    def terms(row):
        k = jnp.concatenate([khat[t, pl.ds(row, 1), :] for t in range(steps)], axis=0)
        k_high = k.astype(BF16).astype(F32)
        k = jnp.concatenate([k_high, k - k_high], axis=0).T.astype(BF16)
        v = jnp.concatenate([wide_v[t, pl.ds(row, 1), :] for t in range(steps)], axis=0)
        f = decay[pl.ds(row, 1), :]
        return k, jnp.concatenate([v, v], axis=0).astype(BF16), jnp.concatenate([f] * (dv // f.shape[1]), axis=1)

    index = lax.broadcasted_iota(jnp.int32, (rows, 1), 0)
    norm = jnp.concatenate([normalizer[b] for b in range(rows)], axis=0)
    for j in range(2):
        norm = jnp.where(index == slots[0, j], back[steps * j : steps * j + 1, dv:], norm)
    f = decay[...]
    norm = jnp.concatenate([f] * (dk // f.shape[1]), axis=1) * norm
    for t in range(steps):
        norm = norm + khat[t]
    for b in range(rows):
        norm_done[b] = norm[b : b + 1, :]
    norm_out = pltpu.make_async_copy(norm_done, new_norm, sems.at[rows])
    norm_out.start()

    @pl.loop(0, rows)
    def _(row):
        k, v, f = terms(row)
        for start in range(0, dv, width):
            at = pl.ds(start, width)
            done[row, :, at] = f[:, start : start + width] * memory[row, :, at] + dot(k, v[:, start : start + width])

        @pl.when(row == slots[0, 0])
        def _():
            done[row, 0:cut, :] = f * head[...] + dot(k[:cut], v)

        leave(row).start()

    k, v, f = terms(slots[0, 0])
    add[0 : dk - cut, :] = dot(k[cut:], v)
    keep[0:4, :] = jnp.concatenate([f] * 4, axis=0)
    k, v, f = terms(slots[0, 1])
    add[dk - cut :, :] = dot(k, v)
    keep[4:8, :] = jnp.concatenate([f] * 4, axis=0)
    norm_out.wait()
    for row in range(rows):
        leave(row).wait()


def update(slots, khat, decay, values, memory, head, normalizer, back):
    steps, rows, dk = khat.shape
    dv, tail = memory.shape[2], 2 * dk - head.shape[0]
    return pl.pallas_call(
        update_kernel,
        in_specs=[SMEM] + [VMEM] * 7,
        out_specs=[ANY, ANY, VMEM, VMEM, SMEM],
        out_shape=[
            pltpu.HBM(memory.shape, F32),
            pltpu.HBM(normalizer.shape, F32),
            pltpu.VMEM((tail, dv), F32),
            pltpu.VMEM((8, dv), F32),
            pltpu.SMEM(slots.shape, slots.dtype),
        ],
        scratch_shapes=[
            pltpu.VMEM(values.shape, F32),
            pltpu.VMEM(memory.shape, F32),
            pltpu.VMEM(normalizer.shape, F32),
            pltpu.SemaphoreType.DMA((rows + 1,)),
        ],
        compiler_params=LIMIT,
        cost_estimate=cost(UPDATE),
        name="update",
    )(slots, khat, decay, values, memory, head, normalizer, back)


def project_kernel(
    place, slots, active, queries, ogate, normalizer, prod, top, under, reach, back, weight, after,
    o0, o1, o2, o3, hidden,
):
    steps, rows, dk = queries.shape
    dv, cols = weight.shape[0], o0.shape[2]
    live = column((active[...] == 1).astype(F32)) > 0.0
    index = lax.broadcasted_iota(jnp.int32, (rows, 1), 0)
    moved = [index == slots[0, j] for j in range(2)]
    norm = jnp.concatenate([normalizer[b] for b in range(rows)], axis=0)
    for j in range(2):
        norm = jnp.where(moved[j], back[steps * j : steps * j + 1, dv:], norm)
    for t in range(steps):
        cell = prod[t]
        for j in range(2):
            cell = jnp.where(moved[j], back[j * steps + t : j * steps + t + 1, :dv], cell)
        factor = reach[t]
        below = under[t] + factor * jnp.sum(norm * queries[t].astype(F32), axis=1, keepdims=True)
        below = jnp.maximum(jnp.abs(below), 1.0)
        factor, below = (jnp.concatenate([x] * (dv // x.shape[1]), axis=1) for x in (factor, below))
        out = (factor * cell + top[t]) / below * jax.nn.sigmoid(ogate[t].astype(F32))
        hidden[t * rows : (t + 1) * rows, :] = jnp.where(live, out, 0.0)

    h = hidden[...].astype(BF16)

    @pl.loop(0, 4)
    def _(m):
        r = []
        for p in range(2):
            at = pl.ds(pl.multiple_of(lax.bitwise_xor(place[0], 2 * m + p) * cols, cols), cols)
            r.append(dot(h, weight[:, at]))
        for n, out in enumerate((o0, o1, o2, o3)):

            @pl.when(m == n)
            def _(out=out):
                out[0] = r[0]
                out[1] = r[1]


def project(place, slots, active, queries, ogate, normalizer, prod, top, under, reach, back, weight, after):
    steps, rows, _ = queries.shape
    dv, width = weight.shape
    return pl.pallas_call(
        project_kernel,
        in_specs=[SMEM, SMEM] + [VMEM] * 10 + [ANY],
        out_specs=[VMEM] * 4,
        out_shape=[pltpu.VMEM((2, steps * rows, width // 8), F32)] * 4,
        scratch_shapes=[pltpu.VMEM((steps * rows, dv), F32)],
        compiler_params=LIMIT,
        cost_estimate=FREE,
        name="project",
    )(place, slots, active, queries, ogate, normalizer, prod, top, under, reach, back, weight, after)


def merge_kernel(r3, r2, r1, o0, after, own, other):
    own[...] = o0[0] + r1[0] + (r2[0] + r3[0])
    other[...] = o0[1] + r1[1] + (r2[1] + r3[1])


def merge(r3, r2, r1, o0, after):
    return pl.pallas_call(
        merge_kernel,
        in_specs=[VMEM] * 4 + [ANY],
        out_specs=[VMEM] * 2,
        out_shape=[pltpu.VMEM(o0.shape[1:], F32)] * 2,
        compiler_params=LIMIT,
        cost_estimate=FREE,
        name="merge",
    )(r3, r2, r1, o0, after)


def finish_kernel(slots, tail, add, keep, tokens, own, z, former, new, mixed, done, mixed_done, sems):
    dk, rest = new.shape[1], new.shape[1] * 2 - tail.shape[0]
    steps, rows, _ = tokens.shape
    outs = [pltpu.make_async_copy(mixed_done, mixed, sems.at[0])]
    total = own[...] + z[...]
    for t in range(steps):
        mixed_done[t] = (tokens[t].astype(F32) + total[t * rows : (t + 1) * rows]).astype(BF16)
    outs[0].start()
    size = rest
    for i in range(tail.shape[0] // size):
        j, row = divmod(i * size + dk - rest, dk)
        at = pl.ds(i * size, size)
        done[at, :] = keep[4 * j : 4 * j + 1, :] * tail[at, :] + add[at, :]
        outs.append(pltpu.make_async_copy(done.at[at], new.at[slots[0, j], pl.ds(row, size)], sems.at[1 + i]))
        outs[-1].start()
    for c in outs:
        c.wait()


def finish(slots, tail, add, keep, tokens, own, z, former):
    return pl.pallas_call(
        finish_kernel,
        in_specs=[SMEM] + [VMEM] * 6 + [ANY],
        out_specs=[ANY, ANY],
        out_shape=[pltpu.HBM(former.shape, F32), pltpu.HBM(tokens.shape, BF16)],
        scratch_shapes=[
            pltpu.VMEM(tail.shape, F32),
            pltpu.VMEM(tokens.shape, BF16),
            pltpu.SemaphoreType.DMA((1 + tail.shape[0] // (2 * former.shape[1] - tail.shape[0]),)),
        ],
        input_output_aliases={7: 0},
        compiler_params=LIMIT,
        cost_estimate=FREE,
        name="finish",
    )(slots, tail, add, keep, tokens, own, z, former)


def per_device(
    memory,
    normalizer,
    queries,
    keys,
    values,
    igate,
    fgate,
    ogate,
    out_weight,
    tokens,
    active,
    pair_mask,
    swap_slots,
):
    steps, rows = queries.shape[0], queries.shape[1]
    groups, heads = lax.axis_size("group"), lax.axis_size("head")
    memory = memory.reshape(rows, *memory.shape[2:])
    queries, keys, values, ogate = (x.reshape(steps, rows, x.shape[3]) for x in (queries, keys, values, ogate))
    igate, fgate = igate.reshape(steps, 1, rows), fgate.reshape(steps, 1, rows)
    active = active.reshape(1, rows)
    weight = out_weight.reshape(out_weight.shape[1:])
    place = lax.axis_index("head").astype(jnp.int32).reshape(1)
    head, tail, asked, norms, core, rest = leave(swap_slots, pair_mask, memory, normalizer, queries)

    def other(*parts):
        return tuple(lax.ppermute(x, "group", [(s, s ^ 1) for s in range(groups)]) for x in parts)

    head, tail, norms = lax.cond(core[0] == 1, other, lambda *parts: parts, head, tail, norms)

    def branch(rest):
        def swap(x):
            return lax.ppermute(x, "group", [(s, s ^ (2 * rest)) for s in range(groups)]) if rest else x

        def across(x, bits):
            return lax.ppermute(x, "head", [(s, s ^ bits) for s in range(heads)])

        def run(*_):
            asked_in = swap(asked)
            first = hold(head, asked)
            head_in = swap(first)
            khat, decay, top, under, reach, token = weigh(igate, fgate, active, queries, keys, values)
            reply, tail_on = answer(first, tail, asked_in, norms, token)
            back = swap(reply)
            tail_in = swap(tail_on)
            prod = products(queries, memory)
            o0, o1, o2, o3 = project(
                place, swap_slots, active, queries, ogate, normalizer, prod, top, under, reach, back, weight, head_in
            )
            r3, r2, r1 = across(o3, 6), across(o2, 4), across(o1, 2)
            new, new_norm, add, keep, where = update(swap_slots, khat, decay, values, memory, head_in, normalizer, back)
            own, other = merge(r3, r2, r1, o0, new)
            z = across(other, 1)
            new, mixed = finish(where, tail_in, add, keep, tokens, own, z, new)
            return new, new_norm, mixed

        return run

    new, new_norm, mixed = lax.switch(rest[0], [branch(rest) for rest in range(groups // 2)])
    return new.reshape(rows, 1, *new.shape[1:]), new_norm, mixed


def solution(mesh):
    placed = (
        P("group", "head", None, None),
        P("group", "head", None),
        P(None, "group", "head", None),
        P(None, "group", "head", None),
        P(None, "group", "head", None),
        P(None, "group", "head"),
        P(None, "group", "head"),
        P(None, "group", "head", None),
        P("head", None, None),
        P(None, "group", "head"),
        P("group"),
        P(),
        P("group", None),
    )
    return jax.shard_map(
        per_device,
        mesh=mesh,
        in_specs=placed,
        out_specs=(
            P("group", "head", None, None),
            P("group", "head", None),
            P(None, "group", "head"),
        ),
        check_vma=False,
    )
```

```python
import functools

import jax
import jax.numpy as jnp
from jax import lax
from jax.experimental import pallas as pl
from jax.experimental.pallas import tpu as pltpu
from jax.sharding import PartitionSpec as P

F32 = jnp.float32
BF16 = jnp.bfloat16
VMEM = pl.BlockSpec(memory_space=pltpu.VMEM)
SMEM = pl.BlockSpec(memory_space=pltpu.SMEM)
ANY = pl.BlockSpec(memory_space=pl.ANY)
HBM = pl.BlockSpec(memory_space=pltpu.HBM)


def cost(size):
    return pl.CostEstimate(flops=size, bytes_accessed=size, transcendentals=0)


FREE = cost(0)
LIMIT = pltpu.CompilerParams(vmem_limit_bytes=16 * 2**20)
PRODUCTS, UPDATE = 10**10, 0


def halves(x):
    high = x.astype(BF16)
    return high, (x - high.astype(F32)).astype(BF16)


def dot(a, b, contract=1):
    return lax.dot_general(a, b, (((contract,), (0,)), ((), ())), preferred_element_type=F32)


def column(row):
    n = row.shape[1]
    eye = lax.broadcasted_iota(jnp.int32, (n, n), 0) == lax.broadcasted_iota(jnp.int32, (n, n), 1)
    return jnp.sum(jnp.where(eye, jnp.broadcast_to(row, (n, n)), 0.0), axis=1, keepdims=True)


def gates(igate, fgate, active):
    live = active[...] == 1
    forget, inflow = [], []
    for t in range(igate.shape[0]):
        forget.append(column(jnp.where(live, jax.nn.sigmoid(fgate[t]), 1.0)))
        inflow.append(column(jnp.where(live, jnp.exp(igate[t]), 0.0)))
    return forget, inflow, column(live.astype(F32))


def leave_kernel(
    slots_in, mask_in, memory, normalizer, queries, head, tail, asked, norms, core, rest,
    slots, mask, raw, norm, wide, sems,
):
    steps, rows = asked.shape[0] // 2, norm.shape[0]
    find = pltpu.make_async_copy(slots_in, slots, sems.at[5])
    find_mask = pltpu.make_async_copy(mask_in, mask, sems.at[6])
    find.start()
    find_mask.start()
    loads = [pltpu.make_async_copy(queries, raw, sems.at[0]), pltpu.make_async_copy(normalizer, norm, sems.at[1])]
    for c in loads:
        c.start()
    find.wait()
    cut, dk = head.shape[0], memory.shape[1]
    one, two = memory.at[slots[0, 0]], memory.at[slots[0, 1]]
    cells = [
        pltpu.make_async_copy(one.at[pl.ds(0, cut)], head, sems.at[2]),
        pltpu.make_async_copy(one.at[pl.ds(cut, dk - cut)], tail.at[pl.ds(0, dk - cut)], sems.at[3]),
        pltpu.make_async_copy(two, tail.at[pl.ds(dk - cut, dk)], sems.at[4]),
    ]
    for c in cells:
        c.start()
    find_mask.wait()
    core[0] = lax.bitwise_and(mask[0], 1)
    rest[0] = lax.shift_right_logical(mask[0], 1)
    for c in loads:
        c.wait()
    wide[...] = raw[...].astype(F32)
    for j in range(2):
        for t in range(steps):
            asked[pl.ds(j * steps + t, 1), :] = wide[pl.ds(t * rows + slots[0, j], 1), :]
    norms[...] = jnp.concatenate([norm[slots[0, j]] for j in (0, 1) for _ in range(steps)], axis=0)
    for c in cells:
        c.wait()


def leave(slots, mask, memory, normalizer, queries):
    _, dk, dv = memory.shape
    steps, rows, _ = queries.shape
    cut = dk // 2
    return pl.pallas_call(
        leave_kernel,
        in_specs=[HBM] * 2 + [ANY] * 3,
        out_specs=[ANY, ANY, VMEM, VMEM, SMEM, SMEM],
        out_shape=[
            jax.ShapeDtypeStruct((cut, dv), F32),
            jax.ShapeDtypeStruct((2 * dk - cut, dv), F32),
            jax.ShapeDtypeStruct((2 * steps, dk), F32),
            jax.ShapeDtypeStruct((2 * steps, dk), F32),
            pltpu.SMEM((1,), jnp.int32),
            pltpu.SMEM((1,), jnp.int32),
        ],
        scratch_shapes=[
            pltpu.SMEM(slots.shape, slots.dtype),
            pltpu.SMEM(mask.shape, mask.dtype),
            pltpu.VMEM((steps * rows, dk), queries.dtype),
            pltpu.VMEM(normalizer.shape, F32),
            pltpu.VMEM((steps * rows, dk), F32),
            pltpu.SemaphoreType.DMA((7,)),
        ],
        compiler_params=LIMIT,
        cost_estimate=FREE,
        name="leave",
    )(slots, mask, memory, normalizer, queries.reshape(steps * rows, dk))


def hold_kernel(x, after, out):
    pass


def hold(x, after):
    return pl.pallas_call(
        hold_kernel,
        in_specs=[VMEM, ANY],
        out_specs=VMEM,
        out_shape=jax.ShapeDtypeStruct(x.shape, x.dtype),
        input_output_aliases={0: 0},
        compiler_params=LIMIT,
        cost_estimate=FREE,
        name="hold",
    )(x, after)


def answer_kernel(head, tail, asked, norms, after, out, tail_on):
    steps = asked.shape[0] // 2
    cut, dk = head.shape[0], asked.shape[1]
    q = asked[...].astype(BF16)
    dv = head.shape[1]
    out[:, dv:] = norms[...]
    first = lax.broadcasted_iota(jnp.int32, (2 * steps, 1), 0) < steps
    parts = ((head, 0, 0), (tail, 0, cut), (tail, dk - cut, 0), (tail, dk, cut))

    @pl.loop(0, dv // 256)
    def _(i):
        at = pl.ds(pl.multiple_of(i * 256, 256), 256)
        r = []
        for x, start, k in parts:
            high, low = halves(x[pl.ds(start, cut), at])
            r.append(dot(q[:, k : k + cut], high) + dot(q[:, k : k + cut], low))
        out[:, at] = jnp.where(first, r[0] + r[1], r[2] + r[3])


def answer(head, tail, asked, norms, after):
    return pl.pallas_call(
        answer_kernel,
        in_specs=[VMEM] * 5,
        out_specs=[VMEM, VMEM],
        out_shape=[
            pltpu.VMEM((asked.shape[0], head.shape[1] + asked.shape[1]), F32),
            jax.ShapeDtypeStruct(tail.shape, F32),
        ],
        input_output_aliases={1: 1},
        compiler_params=LIMIT,
        cost_estimate=FREE,
        name="answer",
    )(head, tail, asked, norms, after)


def weigh_kernel(igate, fgate, active, queries, keys, values, khat, decay, top, under, reach, token):
    token[...] = jnp.zeros_like(token)
    steps, rows, dk = keys.shape
    forget, inflow, _ = gates(igate, fgate, active)
    k = [keys[t].astype(F32) for t in range(steps)]
    weight = jnp.ones_like(forget[0])
    for t in reversed(range(steps)):
        khat[t] = (weight * inflow[t]) * k[t]
        weight = weight * forget[t]
    decay[...] = jnp.broadcast_to(weight, decay.shape)
    beta, so_far = [], jnp.ones_like(forget[0])
    for t in range(steps):
        q = queries[t].astype(F32) * (dk**-0.5)
        beta = [b * forget[t] for b in beta] + [inflow[t]]
        so_far = so_far * forget[t]
        above, below = 0.0, 0.0
        for s in range(t + 1):
            share = beta[s] * jnp.sum(k[s] * q, axis=1, keepdims=True)
            above = above + share * values[s].astype(F32)
            below = below + share
        top[t] = above
        under[t] = jnp.broadcast_to(below, under.shape[1:])
        reach[t] = jnp.broadcast_to(so_far * (dk**-0.5), reach.shape[1:])


def weigh(igate, fgate, active, queries, keys, values):
    steps, rows, dk = keys.shape
    dv = values.shape[2]
    shapes = ((steps, rows, dk), (rows, 128), (steps, rows, dv), (steps, rows, 128), (steps, rows, 128), (8, 128))
    return pl.pallas_call(
        weigh_kernel,
        in_specs=[VMEM] * 6,
        out_specs=[VMEM] * len(shapes),
        out_shape=[pltpu.VMEM(x, F32) for x in shapes],
        compiler_params=LIMIT,
        cost_estimate=FREE,
        name="weigh",
    )(igate, fgate, active, queries, keys, values)


def products_kernel(queries, memory, prod, wide_q):
    steps, rows, _ = queries.shape
    wide_q[...] = queries[...].astype(F32)

    @pl.loop(0, rows, unroll=2)
    def _(row):
        q = jnp.concatenate([wide_q[t, pl.ds(row, 1), :] for t in range(steps)], axis=0)
        q = jnp.concatenate([q, q], axis=0).astype(BF16)
        high, low = halves(memory[row])
        r = dot(q, high) + dot(q, low)
        for t in range(steps):
            prod[t, pl.ds(row, 1), :] = r[t : t + 1, :]


def products(queries, memory):
    steps, rows, dk = queries.shape
    return pl.pallas_call(
        products_kernel,
        in_specs=[VMEM] * 2,
        out_specs=VMEM,
        out_shape=pltpu.VMEM((steps, rows, memory.shape[2]), F32),
        scratch_shapes=[pltpu.VMEM((steps, rows, dk), F32)],
        compiler_params=LIMIT,
        cost_estimate=cost(PRODUCTS),
        name="products",
    )(queries, memory)


def update_kernel(slots, khat, decay, values, memory, head, normalizer, back, new, new_norm, add, keep, where, wide_v, done, norm_done, sems):
    steps, rows, dk = khat.shape
    dv, cut = values.shape[2], head.shape[0]
    width = 256
    wide_v[...] = values[...].astype(F32)
    for j in range(2):
        where[0, j] = slots[0, j]

    def leave(row):
        return pltpu.make_async_copy(done.at[row], new.at[row], sems.at[row])

    def terms(row):
        k = jnp.concatenate([khat[t, pl.ds(row, 1), :] for t in range(steps)], axis=0)
        k_high = k.astype(BF16).astype(F32)
        k = jnp.concatenate([k_high, k - k_high], axis=0).T.astype(BF16)
        v = jnp.concatenate([wide_v[t, pl.ds(row, 1), :] for t in range(steps)], axis=0)
        f = decay[pl.ds(row, 1), :]
        return k, jnp.concatenate([v, v], axis=0).astype(BF16), jnp.concatenate([f] * (dv // f.shape[1]), axis=1)

    index = lax.broadcasted_iota(jnp.int32, (rows, 1), 0)
    norm = jnp.concatenate([normalizer[b] for b in range(rows)], axis=0)
    for j in range(2):
        norm = jnp.where(index == slots[0, j], back[steps * j : steps * j + 1, dv:], norm)
    f = decay[...]
    norm = jnp.concatenate([f] * (dk // f.shape[1]), axis=1) * norm
    for t in range(steps):
        norm = norm + khat[t]
    for b in range(rows):
        norm_done[b] = norm[b : b + 1, :]
    norm_out = pltpu.make_async_copy(norm_done, new_norm, sems.at[rows])
    norm_out.start()

    @pl.loop(0, rows)
    def _(row):
        k, v, f = terms(row)
        for start in range(0, dv, width):
            at = pl.ds(start, width)
            done[row, :, at] = f[:, start : start + width] * memory[row, :, at] + dot(k, v[:, start : start + width])

        @pl.when(row == slots[0, 0])
        def _():
            done[row, 0:cut, :] = f * head[...] + dot(k[:cut], v)

        leave(row).start()

    k, v, f = terms(slots[0, 0])
    add[0 : dk - cut, :] = dot(k[cut:], v)
    keep[0:4, :] = jnp.concatenate([f] * 4, axis=0)
    k, v, f = terms(slots[0, 1])
    add[dk - cut :, :] = dot(k, v)
    keep[4:8, :] = jnp.concatenate([f] * 4, axis=0)
    norm_out.wait()
    for row in range(rows):
        leave(row).wait()


def update(slots, khat, decay, values, memory, head, normalizer, back):
    steps, rows, dk = khat.shape
    dv, tail = memory.shape[2], 2 * dk - head.shape[0]
    return pl.pallas_call(
        update_kernel,
        in_specs=[SMEM] + [VMEM] * 7,
        out_specs=[ANY, ANY, VMEM, VMEM, SMEM],
        out_shape=[
            pltpu.HBM(memory.shape, F32),
            pltpu.HBM(normalizer.shape, F32),
            pltpu.VMEM((tail, dv), F32),
            pltpu.VMEM((8, dv), F32),
            pltpu.SMEM(slots.shape, slots.dtype),
        ],
        scratch_shapes=[
            pltpu.VMEM(values.shape, F32),
            pltpu.VMEM(memory.shape, F32),
            pltpu.VMEM(normalizer.shape, F32),
            pltpu.SemaphoreType.DMA((rows + 1,)),
        ],
        compiler_params=LIMIT,
        cost_estimate=cost(UPDATE),
        name="update",
    )(slots, khat, decay, values, memory, head, normalizer, back)


def project_kernel(
    place, slots, active, queries, ogate, normalizer, prod, top, under, reach, back, weight, after,
    o0, o1, o2, o3, hidden,
):
    steps, rows, dk = queries.shape
    dv, cols = weight.shape[0], o0.shape[2]
    live = column((active[...] == 1).astype(F32)) > 0.0
    index = lax.broadcasted_iota(jnp.int32, (rows, 1), 0)
    moved = [index == slots[0, j] for j in range(2)]
    norm = jnp.concatenate([normalizer[b] for b in range(rows)], axis=0)
    for j in range(2):
        norm = jnp.where(moved[j], back[steps * j : steps * j + 1, dv:], norm)
    for t in range(steps):
        cell = prod[t]
        for j in range(2):
            cell = jnp.where(moved[j], back[j * steps + t : j * steps + t + 1, :dv], cell)
        factor = reach[t]
        below = under[t] + factor * jnp.sum(norm * queries[t].astype(F32), axis=1, keepdims=True)
        below = jnp.maximum(jnp.abs(below), 1.0)
        factor, below = (jnp.concatenate([x] * (dv // x.shape[1]), axis=1) for x in (factor, below))
        out = (factor * cell + top[t]) / below * jax.nn.sigmoid(ogate[t].astype(F32))
        hidden[t * rows : (t + 1) * rows, :] = jnp.where(live, out, 0.0)

    h = hidden[...].astype(BF16)

    @pl.loop(0, 4)
    def _(m):
        r = []
        for p in range(2):
            at = pl.ds(pl.multiple_of(lax.bitwise_xor(place[0], 2 * m + p) * cols, cols), cols)
            r.append(dot(h, weight[:, at]))
        for n, out in enumerate((o0, o1, o2, o3)):

            @pl.when(m == n)
            def _(out=out):
                out[0] = r[0]
                out[1] = r[1]


def project(place, slots, active, queries, ogate, normalizer, prod, top, under, reach, back, weight, after):
    steps, rows, _ = queries.shape
    dv, width = weight.shape
    return pl.pallas_call(
        project_kernel,
        in_specs=[SMEM, SMEM] + [VMEM] * 10 + [ANY],
        out_specs=[VMEM] * 4,
        out_shape=[pltpu.VMEM((2, steps * rows, width // 8), F32)] * 4,
        scratch_shapes=[pltpu.VMEM((steps * rows, dv), F32)],
        compiler_params=LIMIT,
        cost_estimate=FREE,
        name="project",
    )(place, slots, active, queries, ogate, normalizer, prod, top, under, reach, back, weight, after)


def merge_kernel(r3, r2, r1, o0, after, own, other):
    own[...] = o0[0] + r1[0] + (r2[0] + r3[0])
    other[...] = o0[1] + r1[1] + (r2[1] + r3[1])


def merge(r3, r2, r1, o0, after):
    return pl.pallas_call(
        merge_kernel,
        in_specs=[VMEM] * 4 + [ANY],
        out_specs=[VMEM] * 2,
        out_shape=[pltpu.VMEM(o0.shape[1:], F32)] * 2,
        compiler_params=LIMIT,
        cost_estimate=FREE,
        name="merge",
    )(r3, r2, r1, o0, after)


def finish_kernel(slots, tail, add, keep, tokens, own, z, former, new, mixed, done, mixed_done, sems):
    dk, rest = new.shape[1], new.shape[1] * 2 - tail.shape[0]
    outs = [pltpu.make_async_copy(mixed_done, mixed, sems.at[0])]
    mixed_done[...] = (tokens[...].astype(F32) + (own[...] + z[...])).astype(BF16)
    outs[0].start()
    size = rest
    for i in range(tail.shape[0] // size):
        j, row = divmod(i * size + dk - rest, dk)
        at = pl.ds(i * size, size)
        done[at, :] = keep[4 * j : 4 * j + 1, :] * tail[at, :] + add[at, :]
        outs.append(pltpu.make_async_copy(done.at[at], new.at[slots[0, j], pl.ds(row, size)], sems.at[1 + i]))
        outs[-1].start()
    for c in outs:
        c.wait()


def finish(slots, tail, add, keep, tokens, own, z, former):
    return pl.pallas_call(
        finish_kernel,
        in_specs=[SMEM] + [VMEM] * 6 + [ANY],
        out_specs=[ANY, ANY],
        out_shape=[pltpu.HBM(former.shape, F32), pltpu.HBM(tokens.shape, BF16)],
        scratch_shapes=[
            pltpu.VMEM(tail.shape, F32),
            pltpu.VMEM(tokens.shape, BF16),
            pltpu.SemaphoreType.DMA((1 + tail.shape[0] // (2 * former.shape[1] - tail.shape[0]),)),
        ],
        input_output_aliases={7: 0},
        compiler_params=LIMIT,
        cost_estimate=FREE,
        name="finish",
    )(slots, tail, add, keep, tokens, own, z, former)


def per_device(
    memory,
    normalizer,
    queries,
    keys,
    values,
    igate,
    fgate,
    ogate,
    out_weight,
    tokens,
    active,
    pair_mask,
    swap_slots,
):
    steps, rows = queries.shape[0], queries.shape[1]
    groups, heads = lax.axis_size("group"), lax.axis_size("head")
    memory = memory.reshape(rows, *memory.shape[2:])
    queries, keys, values, ogate = (x.reshape(steps, rows, x.shape[3]) for x in (queries, keys, values, ogate))
    igate, fgate = igate.reshape(steps, 1, rows), fgate.reshape(steps, 1, rows)
    active = active.reshape(1, rows)
    weight = out_weight.reshape(out_weight.shape[1:])
    place = lax.axis_index("head").astype(jnp.int32).reshape(1)
    head, tail, asked, norms, core, rest = leave(swap_slots, pair_mask, memory, normalizer, queries)

    def other(*parts):
        return tuple(lax.ppermute(x, "group", [(s, s ^ 1) for s in range(groups)]) for x in parts)

    head, tail, norms = lax.cond(core[0] == 1, other, lambda *parts: parts, head, tail, norms)

    def branch(rest):
        def swap(x):
            return lax.ppermute(x, "group", [(s, s ^ (2 * rest)) for s in range(groups)]) if rest else x

        def across(x, bits):
            return lax.ppermute(x, "head", [(s, s ^ bits) for s in range(heads)])

        def run(*_):
            asked_in = swap(asked)
            first = hold(head, asked)
            head_in = swap(first)
            khat, decay, top, under, reach, token = weigh(igate, fgate, active, queries, keys, values)
            reply, tail_on = answer(first, tail, asked_in, norms, token)
            back = swap(reply)
            tail_in = swap(tail_on)
            prod = products(queries, memory)
            o0, o1, o2, o3 = project(
                place, swap_slots, active, queries, ogate, normalizer, prod, top, under, reach, back, weight, head_in
            )
            r3, r2, r1 = across(o3, 6), across(o2, 4), across(o1, 2)
            new, new_norm, add, keep, where = update(swap_slots, khat, decay, values, memory, head_in, normalizer, back)
            own, beside = merge(r3, r2, r1, o0, new)
            z = across(beside, 1)
            new, mixed = finish(where, tail_in, add, keep, tokens.reshape(own.shape), own, z, new)
            return new, new_norm, mixed

        return run

    new, new_norm, mixed = lax.switch(rest[0], [branch(rest) for rest in range(groups // 2)])
    return new.reshape(rows, 1, *new.shape[1:]), new_norm, mixed.reshape(tokens.shape)


def solution(mesh):
    placed = (
        P("group", "head", None, None),
        P("group", "head", None),
        P(None, "group", "head", None),
        P(None, "group", "head", None),
        P(None, "group", "head", None),
        P(None, "group", "head"),
        P(None, "group", "head"),
        P(None, "group", "head", None),
        P("head", None, None),
        P(None, "group", "head"),
        P("group"),
        P(),
        P("group", None),
    )
    return jax.shard_map(
        per_device,
        mesh=mesh,
        in_specs=placed,
        out_specs=(
            P("group", "head", None, None),
            P("group", "head", None),
            P(None, "group", "head"),
        ),
        check_vma=False,
    )
```

```python
import functools

import jax
import jax.numpy as jnp
from jax import lax
from jax.experimental import pallas as pl
from jax.experimental.pallas import tpu as pltpu
from jax.sharding import PartitionSpec as P

F32 = jnp.float32
BF16 = jnp.bfloat16
VMEM = pl.BlockSpec(memory_space=pltpu.VMEM)
SMEM = pl.BlockSpec(memory_space=pltpu.SMEM)
ANY = pl.BlockSpec(memory_space=pl.ANY)
HBM = pl.BlockSpec(memory_space=pltpu.HBM)


def cost(size):
    return pl.CostEstimate(flops=size, bytes_accessed=size, transcendentals=0)


FREE = cost(0)
LIMIT = pltpu.CompilerParams(vmem_limit_bytes=16 * 2**20)
PRODUCTS, UPDATE = 10**10, 0


def halves(x):
    high = x.astype(BF16)
    return high, (x - high.astype(F32)).astype(BF16)


def dot(a, b, contract=1):
    return lax.dot_general(a, b, (((contract,), (0,)), ((), ())), preferred_element_type=F32)


def column(row):
    n = row.shape[1]
    eye = lax.broadcasted_iota(jnp.int32, (n, n), 0) == lax.broadcasted_iota(jnp.int32, (n, n), 1)
    return jnp.sum(jnp.where(eye, jnp.broadcast_to(row, (n, n)), 0.0), axis=1, keepdims=True)


def gates(igate, fgate, active):
    live = active[...] == 1
    forget, inflow = [], []
    for t in range(igate.shape[0]):
        forget.append(column(jnp.where(live, jax.nn.sigmoid(fgate[t]), 1.0)))
        inflow.append(column(jnp.where(live, jnp.exp(igate[t]), 0.0)))
    return forget, inflow, column(live.astype(F32))


def leave_kernel(
    slots_in, mask_in, memory, normalizer, queries, head, tail, asked, norms, core, rest,
    slots, mask, raw, norm, wide, sems,
):
    steps, rows = asked.shape[0] // 2, norm.shape[0]
    find = pltpu.make_async_copy(slots_in, slots, sems.at[5])
    find_mask = pltpu.make_async_copy(mask_in, mask, sems.at[6])
    find.start()
    find_mask.start()
    loads = [pltpu.make_async_copy(queries, raw, sems.at[0]), pltpu.make_async_copy(normalizer, norm, sems.at[1])]
    for c in loads:
        c.start()
    find.wait()
    cut, dk = head.shape[0], memory.shape[1]
    one, two = memory.at[slots[0, 0]], memory.at[slots[0, 1]]
    cells = [
        pltpu.make_async_copy(one.at[pl.ds(0, cut)], head, sems.at[2]),
        pltpu.make_async_copy(one.at[pl.ds(cut, dk - cut)], tail.at[pl.ds(0, dk - cut)], sems.at[3]),
        pltpu.make_async_copy(two, tail.at[pl.ds(dk - cut, dk)], sems.at[4]),
    ]
    for c in cells:
        c.start()
    find_mask.wait()
    core[0] = lax.bitwise_and(mask[0], 1)
    rest[0] = lax.shift_right_logical(mask[0], 1)
    for c in loads:
        c.wait()
    wide[...] = raw[...].astype(F32)
    for j in range(2):
        for t in range(steps):
            asked[pl.ds(j * steps + t, 1), :] = wide[pl.ds(t * rows + slots[0, j], 1), :]
    norms[...] = jnp.concatenate([norm[slots[0, j]] for j in (0, 1) for _ in range(steps)], axis=0)
    for c in cells:
        c.wait()


def leave(slots, mask, memory, normalizer, queries):
    _, dk, dv = memory.shape
    steps, rows, _ = queries.shape
    cut = dk // 2
    return pl.pallas_call(
        leave_kernel,
        in_specs=[HBM] * 2 + [ANY] * 3,
        out_specs=[ANY, ANY, VMEM, VMEM, SMEM, SMEM],
        out_shape=[
            jax.ShapeDtypeStruct((cut, dv), F32),
            jax.ShapeDtypeStruct((2 * dk - cut, dv), F32),
            jax.ShapeDtypeStruct((2 * steps, dk), F32),
            jax.ShapeDtypeStruct((2 * steps, dk), F32),
            pltpu.SMEM((1,), jnp.int32),
            pltpu.SMEM((1,), jnp.int32),
        ],
        scratch_shapes=[
            pltpu.SMEM(slots.shape, slots.dtype),
            pltpu.SMEM(mask.shape, mask.dtype),
            pltpu.VMEM((steps * rows, dk), queries.dtype),
            pltpu.VMEM(normalizer.shape, F32),
            pltpu.VMEM((steps * rows, dk), F32),
            pltpu.SemaphoreType.DMA((7,)),
        ],
        compiler_params=LIMIT,
        cost_estimate=FREE,
        name="leave",
    )(slots, mask, memory, normalizer, queries.reshape(steps * rows, dk))


def hold_kernel(x, after, out):
    pass


def hold(x, after):
    return pl.pallas_call(
        hold_kernel,
        in_specs=[VMEM, ANY],
        out_specs=VMEM,
        out_shape=jax.ShapeDtypeStruct(x.shape, x.dtype),
        input_output_aliases={0: 0},
        compiler_params=LIMIT,
        cost_estimate=FREE,
        name="hold",
    )(x, after)


def answer_kernel(head, tail, asked, norms, after, out, tail_on):
    steps = asked.shape[0] // 2
    cut, dk = head.shape[0], asked.shape[1]
    q = asked[...].astype(BF16)
    dv = head.shape[1]
    out[:, dv:] = norms[...]
    first = lax.broadcasted_iota(jnp.int32, (2 * steps, 1), 0) < steps
    parts = ((head, 0, 0), (tail, 0, cut), (tail, dk - cut, 0), (tail, dk, cut))

    @pl.loop(0, dv // 256)
    def _(i):
        at = pl.ds(pl.multiple_of(i * 256, 256), 256)
        r = []
        for x, start, k in parts:
            high, low = halves(x[pl.ds(start, cut), at])
            r.append(dot(q[:, k : k + cut], high) + dot(q[:, k : k + cut], low))
        out[:, at] = jnp.where(first, r[0] + r[1], r[2] + r[3])


def answer(head, tail, asked, norms, after):
    return pl.pallas_call(
        answer_kernel,
        in_specs=[VMEM] * 5,
        out_specs=[VMEM, VMEM],
        out_shape=[
            pltpu.VMEM((asked.shape[0], head.shape[1] + asked.shape[1]), F32),
            jax.ShapeDtypeStruct(tail.shape, F32),
        ],
        input_output_aliases={1: 1},
        compiler_params=LIMIT,
        cost_estimate=FREE,
        name="answer",
    )(head, tail, asked, norms, after)


def weigh_kernel(igate, fgate, active, queries, keys, values, khat, decay, top, under, reach, token):
    token[...] = jnp.zeros_like(token)
    steps, rows, dk = keys.shape
    forget, inflow, _ = gates(igate, fgate, active)
    k = [keys[t].astype(F32) for t in range(steps)]
    weight = jnp.ones_like(forget[0])
    for t in reversed(range(steps)):
        khat[t] = (weight * inflow[t]) * k[t]
        weight = weight * forget[t]
    decay[...] = jnp.broadcast_to(weight, decay.shape)
    beta, so_far = [], jnp.ones_like(forget[0])
    for t in range(steps):
        q = queries[t].astype(F32) * (dk**-0.5)
        beta = [b * forget[t] for b in beta] + [inflow[t]]
        so_far = so_far * forget[t]
        above, below = 0.0, 0.0
        for s in range(t + 1):
            share = beta[s] * jnp.sum(k[s] * q, axis=1, keepdims=True)
            above = above + share * values[s].astype(F32)
            below = below + share
        top[t] = above
        under[t] = jnp.broadcast_to(below, under.shape[1:])
        reach[t] = jnp.broadcast_to(so_far * (dk**-0.5), reach.shape[1:])


def weigh(igate, fgate, active, queries, keys, values):
    steps, rows, dk = keys.shape
    dv = values.shape[2]
    shapes = ((steps, rows, dk), (rows, 128), (steps, rows, dv), (steps, rows, 128), (steps, rows, 128), (8, 128))
    return pl.pallas_call(
        weigh_kernel,
        in_specs=[VMEM] * 6,
        out_specs=[VMEM] * len(shapes),
        out_shape=[pltpu.VMEM(x, F32) for x in shapes],
        compiler_params=LIMIT,
        cost_estimate=FREE,
        name="weigh",
    )(igate, fgate, active, queries, keys, values)


def products_kernel(queries, memory, prod, wide_q):
    steps, rows, _ = queries.shape
    wide_q[...] = queries[...].astype(F32)

    @pl.loop(0, rows, unroll=2)
    def _(row):
        q = jnp.concatenate([wide_q[t, pl.ds(row, 1), :] for t in range(steps)], axis=0)
        q = jnp.concatenate([q, q], axis=0).astype(BF16)
        high, low = halves(memory[row])
        r = dot(q, high) + dot(q, low)
        for t in range(steps):
            prod[t, pl.ds(row, 1), :] = r[t : t + 1, :]


def products(queries, memory):
    steps, rows, dk = queries.shape
    return pl.pallas_call(
        products_kernel,
        in_specs=[VMEM] * 2,
        out_specs=VMEM,
        out_shape=pltpu.VMEM((steps, rows, memory.shape[2]), F32),
        scratch_shapes=[pltpu.VMEM((steps, rows, dk), F32)],
        compiler_params=LIMIT,
        cost_estimate=cost(PRODUCTS),
        name="products",
    )(queries, memory)


def update_kernel(slots, khat, decay, values, memory, head, normalizer, back, new, new_norm, add, keep, where, wide_v, done, norm_done, sems):
    steps, rows, dk = khat.shape
    dv, cut = values.shape[2], head.shape[0]
    width = 256
    wide_v[...] = values[...].astype(F32)
    for j in range(2):
        where[0, j] = slots[0, j]

    def leave(row):
        return pltpu.make_async_copy(done.at[row], new.at[row], sems.at[row])

    def terms(row):
        k = jnp.concatenate([khat[t, pl.ds(row, 1), :] for t in range(steps)], axis=0)
        k_high = k.astype(BF16).astype(F32)
        k = jnp.concatenate([k_high, k - k_high], axis=0).T.astype(BF16)
        v = jnp.concatenate([wide_v[t, pl.ds(row, 1), :] for t in range(steps)], axis=0)
        f = decay[pl.ds(row, 1), :]
        return k, jnp.concatenate([v, v], axis=0).astype(BF16), jnp.concatenate([f] * (dv // f.shape[1]), axis=1)

    index = lax.broadcasted_iota(jnp.int32, (rows, 1), 0)
    norm = jnp.concatenate([normalizer[b] for b in range(rows)], axis=0)
    for j in range(2):
        norm = jnp.where(index == slots[0, j], back[steps * j : steps * j + 1, dv:], norm)
    f = decay[...]
    norm = jnp.concatenate([f] * (dk // f.shape[1]), axis=1) * norm
    for t in range(steps):
        norm = norm + khat[t]
    for b in range(rows):
        norm_done[b] = norm[b : b + 1, :]
    norm_out = pltpu.make_async_copy(norm_done, new_norm, sems.at[rows])
    norm_out.start()

    @pl.loop(0, rows)
    def _(row):
        k, v, f = terms(row)
        for start in range(0, dv, width):
            at = pl.ds(start, width)
            done[row, :, at] = f[:, start : start + width] * memory[row, :, at] + dot(k, v[:, start : start + width])

        @pl.when(row == slots[0, 0])
        def _():
            done[row, 0:cut, :] = f * head[...] + dot(k[:cut], v)

        leave(row).start()

    k, v, f = terms(slots[0, 0])
    add[0 : dk - cut, :] = dot(k[cut:], v)
    keep[0:4, :] = jnp.concatenate([f] * 4, axis=0)
    k, v, f = terms(slots[0, 1])
    add[dk - cut :, :] = dot(k, v)
    keep[4:8, :] = jnp.concatenate([f] * 4, axis=0)
    norm_out.wait()
    for row in range(rows):
        leave(row).wait()


def update(slots, khat, decay, values, memory, head, normalizer, back):
    steps, rows, dk = khat.shape
    dv, tail = memory.shape[2], 2 * dk - head.shape[0]
    return pl.pallas_call(
        update_kernel,
        in_specs=[SMEM] + [VMEM] * 7,
        out_specs=[ANY, ANY, VMEM, VMEM, SMEM],
        out_shape=[
            pltpu.HBM(memory.shape, F32),
            pltpu.HBM(normalizer.shape, F32),
            pltpu.VMEM((tail, dv), F32),
            pltpu.VMEM((8, dv), F32),
            pltpu.SMEM(slots.shape, slots.dtype),
        ],
        scratch_shapes=[
            pltpu.VMEM(values.shape, F32),
            pltpu.VMEM(memory.shape, F32),
            pltpu.VMEM(normalizer.shape, F32),
            pltpu.SemaphoreType.DMA((rows + 1,)),
        ],
        compiler_params=LIMIT,
        cost_estimate=cost(UPDATE),
        name="update",
    )(slots, khat, decay, values, memory, head, normalizer, back)


def project_kernel(
    place, slots, active, queries, ogate, normalizer, prod, top, under, reach, back, weight, after,
    o0, o1, o2, o3, hidden,
):
    steps, rows, dk = queries.shape
    dv, cols = weight.shape[0], o0.shape[2]
    live = column((active[...] == 1).astype(F32)) > 0.0
    index = lax.broadcasted_iota(jnp.int32, (rows, 1), 0)
    moved = [index == slots[:, j : j + 1] for j in range(2)]
    norm = jnp.concatenate([normalizer[b] for b in range(rows)], axis=0)
    for j in range(2):
        norm = jnp.where(moved[j], back[steps * j : steps * j + 1, dv:], norm)
    for t in range(steps):
        cell = prod[t]
        for j in range(2):
            cell = jnp.where(moved[j], back[j * steps + t : j * steps + t + 1, :dv], cell)
        factor = reach[t]
        below = under[t] + factor * jnp.sum(norm * queries[t].astype(F32), axis=1, keepdims=True)
        below = jnp.maximum(jnp.abs(below), 1.0)
        factor, below = (jnp.concatenate([x] * (dv // x.shape[1]), axis=1) for x in (factor, below))
        out = (factor * cell + top[t]) / below * jax.nn.sigmoid(ogate[t].astype(F32))
        hidden[t * rows : (t + 1) * rows, :] = jnp.where(live, out, 0.0)

    h = hidden[...].astype(BF16)

    @pl.loop(0, 4)
    def _(m):
        r = []
        for p in range(2):
            at = pl.ds(pl.multiple_of(lax.bitwise_xor(place[0], 2 * m + p) * cols, cols), cols)
            r.append(dot(h, weight[:, at]))
        for n, out in enumerate((o0, o1, o2, o3)):

            @pl.when(m == n)
            def _(out=out):
                out[0] = r[0]
                out[1] = r[1]


def project(place, slots, active, queries, ogate, normalizer, prod, top, under, reach, back, weight, after):
    steps, rows, _ = queries.shape
    dv, width = weight.shape
    return pl.pallas_call(
        project_kernel,
        in_specs=[SMEM] + [VMEM] * 11 + [ANY],
        out_specs=[VMEM] * 4,
        out_shape=[pltpu.VMEM((2, steps * rows, width // 8), F32)] * 4,
        scratch_shapes=[pltpu.VMEM((steps * rows, dv), F32)],
        compiler_params=LIMIT,
        cost_estimate=FREE,
        name="project",
    )(place, slots, active, queries, ogate, normalizer, prod, top, under, reach, back, weight, after)


def merge_kernel(r2, r3, r1, o0, after, own, other):
    own[...] = o0[0] + r1[0] + (r2[0] + r3[0])
    other[...] = o0[1] + r1[1] + (r2[1] + r3[1])


def merge(r2, r3, r1, o0, after):
    return pl.pallas_call(
        merge_kernel,
        in_specs=[VMEM] * 4 + [ANY],
        out_specs=[VMEM] * 2,
        out_shape=[pltpu.VMEM(o0.shape[1:], F32)] * 2,
        compiler_params=LIMIT,
        cost_estimate=FREE,
        name="merge",
    )(r2, r3, r1, o0, after)


def finish_kernel(slots, tail, add, keep, tokens, own, z, former, new, mixed, done, mixed_done, sems):
    dk, rest = new.shape[1], new.shape[1] * 2 - tail.shape[0]
    outs = [pltpu.make_async_copy(mixed_done, mixed, sems.at[0])]
    mixed_done[...] = (tokens[...].astype(F32) + (own[...] + z[...])).astype(BF16)
    outs[0].start()
    size = rest
    for i in range(tail.shape[0] // size):
        j, row = divmod(i * size + dk - rest, dk)
        at = pl.ds(i * size, size)
        done[at, :] = keep[4 * j : 4 * j + 1, :] * tail[at, :] + add[at, :]
        outs.append(pltpu.make_async_copy(done.at[at], new.at[slots[0, j], pl.ds(row, size)], sems.at[1 + i]))
        outs[-1].start()
    for c in outs:
        c.wait()


def finish(slots, tail, add, keep, tokens, own, z, former):
    return pl.pallas_call(
        finish_kernel,
        in_specs=[SMEM] + [VMEM] * 6 + [ANY],
        out_specs=[ANY, ANY],
        out_shape=[pltpu.HBM(former.shape, F32), pltpu.HBM(tokens.shape, BF16)],
        scratch_shapes=[
            pltpu.VMEM(tail.shape, F32),
            pltpu.VMEM(tokens.shape, BF16),
            pltpu.SemaphoreType.DMA((1 + tail.shape[0] // (2 * former.shape[1] - tail.shape[0]),)),
        ],
        input_output_aliases={7: 0},
        compiler_params=LIMIT,
        cost_estimate=FREE,
        name="finish",
    )(slots, tail, add, keep, tokens, own, z, former)


def per_device(
    memory,
    normalizer,
    queries,
    keys,
    values,
    igate,
    fgate,
    ogate,
    out_weight,
    tokens,
    active,
    pair_mask,
    swap_slots,
):
    steps, rows = queries.shape[0], queries.shape[1]
    groups, heads = lax.axis_size("group"), lax.axis_size("head")
    memory = memory.reshape(rows, *memory.shape[2:])
    queries, keys, values, ogate = (x.reshape(steps, rows, x.shape[3]) for x in (queries, keys, values, ogate))
    igate, fgate = igate.reshape(steps, 1, rows), fgate.reshape(steps, 1, rows)
    active = active.reshape(1, rows)
    weight = out_weight.reshape(out_weight.shape[1:])
    place = lax.axis_index("head").astype(jnp.int32).reshape(1)
    head, tail, asked, norms, core, rest = leave(swap_slots, pair_mask, memory, normalizer, queries)

    def other(*parts):
        return tuple(lax.ppermute(x, "group", [(s, s ^ 1) for s in range(groups)]) for x in parts)

    head, tail, norms = lax.cond(core[0] == 1, other, lambda *parts: parts, head, tail, norms)

    def branch(rest):
        def swap(x):
            return lax.ppermute(x, "group", [(s, s ^ (2 * rest)) for s in range(groups)]) if rest else x

        def across(x, bits):
            return lax.ppermute(x, "head", [(s, s ^ bits) for s in range(heads)])

        def run(*_):
            asked_in = swap(asked)
            first = hold(head, asked)
            head_in = swap(first)
            khat, decay, top, under, reach, token = weigh(igate, fgate, active, queries, keys, values)
            reply, tail_on = answer(first, tail, asked_in, norms, token)
            back = swap(reply)
            tail_in = swap(tail_on)
            prod = products(queries, memory)
            o0, o1, o2, o3 = project(
                place, swap_slots, active, queries, ogate, normalizer, prod, top, under, reach, back, weight, head_in
            )
            r2, r3, r1 = across(o2, 4), across(o3, 6), across(o1, 2)
            new, new_norm, add, keep, where = update(swap_slots, khat, decay, values, memory, head_in, normalizer, back)
            own, beside = merge(r2, r3, r1, o0, new)
            z = across(beside, 1)
            new, mixed = finish(where, tail_in, add, keep, tokens.reshape(own.shape), own, z, new)
            return new, new_norm, mixed

        return run

    new, new_norm, mixed = lax.switch(rest[0], [branch(rest) for rest in range(groups // 2)])
    return new.reshape(rows, 1, *new.shape[1:]), new_norm, mixed.reshape(tokens.shape)


def solution(mesh):
    placed = (
        P("group", "head", None, None),
        P("group", "head", None),
        P(None, "group", "head", None),
        P(None, "group", "head", None),
        P(None, "group", "head", None),
        P(None, "group", "head"),
        P(None, "group", "head"),
        P(None, "group", "head", None),
        P("head", None, None),
        P(None, "group", "head"),
        P("group"),
        P(),
        P("group", None),
    )
    return jax.shard_map(
        per_device,
        mesh=mesh,
        in_specs=placed,
        out_specs=(
            P("group", "head", None, None),
            P("group", "head", None),
            P(None, "group", "head"),
        ),
        check_vma=False,
    )
```

```python
import functools

import jax
import jax.numpy as jnp
from jax import lax
from jax.experimental import pallas as pl
from jax.experimental.pallas import tpu as pltpu
from jax.sharding import PartitionSpec as P

F32 = jnp.float32
BF16 = jnp.bfloat16
VMEM = pl.BlockSpec(memory_space=pltpu.VMEM)
SMEM = pl.BlockSpec(memory_space=pltpu.SMEM)
ANY = pl.BlockSpec(memory_space=pl.ANY)
HBM = pl.BlockSpec(memory_space=pltpu.HBM)


def cost(size):
    return pl.CostEstimate(flops=size, bytes_accessed=size, transcendentals=0)


FREE = cost(0)
LIMIT = pltpu.CompilerParams(vmem_limit_bytes=16 * 2**20)
PRODUCTS, UPDATE = 10**10, 0


def halves(x):
    high = x.astype(BF16)
    return high, (x - high.astype(F32)).astype(BF16)


def dot(a, b, contract=1):
    return lax.dot_general(a, b, (((contract,), (0,)), ((), ())), preferred_element_type=F32)


def column(row):
    n = row.shape[1]
    eye = lax.broadcasted_iota(jnp.int32, (n, n), 0) == lax.broadcasted_iota(jnp.int32, (n, n), 1)
    return jnp.sum(jnp.where(eye, jnp.broadcast_to(row, (n, n)), 0.0), axis=1, keepdims=True)


def gates(igate, fgate, active):
    live = active[...] == 1
    forget, inflow = [], []
    for t in range(igate.shape[0]):
        forget.append(column(jnp.where(live, jax.nn.sigmoid(fgate[t]), 1.0)))
        inflow.append(column(jnp.where(live, jnp.exp(igate[t]), 0.0)))
    return forget, inflow, column(live.astype(F32))


def leave_kernel(
    slots_in, mask_in, memory, normalizer, queries, head, tail, asked, norms, core, rest,
    slots, mask, raw, norm, wide, sems,
):
    steps, rows = asked.shape[0] // 2, norm.shape[0]
    find = pltpu.make_async_copy(slots_in, slots, sems.at[5])
    find_mask = pltpu.make_async_copy(mask_in, mask, sems.at[6])
    find.start()
    find_mask.start()
    loads = [pltpu.make_async_copy(queries, raw, sems.at[0]), pltpu.make_async_copy(normalizer, norm, sems.at[1])]
    for c in loads:
        c.start()
    find.wait()
    cut, dk = head.shape[0], memory.shape[1]
    one, two = memory.at[slots[0, 0]], memory.at[slots[0, 1]]
    cells = [
        pltpu.make_async_copy(one.at[pl.ds(0, cut)], head, sems.at[2]),
        pltpu.make_async_copy(one.at[pl.ds(cut, dk - cut)], tail.at[pl.ds(0, dk - cut)], sems.at[3]),
        pltpu.make_async_copy(two, tail.at[pl.ds(dk - cut, dk)], sems.at[4]),
    ]
    for c in cells:
        c.start()
    find_mask.wait()
    core[0] = lax.bitwise_and(mask[0], 1)
    rest[0] = lax.shift_right_logical(mask[0], 1)
    for c in loads:
        c.wait()
    wide[...] = raw[...].astype(F32)
    for j in range(2):
        for t in range(steps):
            asked[pl.ds(j * steps + t, 1), :] = wide[pl.ds(t * rows + slots[0, j], 1), :]
    norms[...] = jnp.concatenate([norm[slots[0, j]] for j in (0, 1) for _ in range(steps)], axis=0)
    for c in cells:
        c.wait()


def leave(slots, mask, memory, normalizer, queries):
    _, dk, dv = memory.shape
    steps, rows, _ = queries.shape
    cut = dk // 2
    return pl.pallas_call(
        leave_kernel,
        in_specs=[HBM] * 2 + [ANY] * 3,
        out_specs=[ANY, ANY, VMEM, VMEM, SMEM, SMEM],
        out_shape=[
            jax.ShapeDtypeStruct((cut, dv), F32),
            jax.ShapeDtypeStruct((2 * dk - cut, dv), F32),
            jax.ShapeDtypeStruct((2 * steps, dk), F32),
            jax.ShapeDtypeStruct((2 * steps, dk), F32),
            pltpu.SMEM((1,), jnp.int32),
            pltpu.SMEM((1,), jnp.int32),
        ],
        scratch_shapes=[
            pltpu.SMEM(slots.shape, slots.dtype),
            pltpu.SMEM(mask.shape, mask.dtype),
            pltpu.VMEM((steps * rows, dk), queries.dtype),
            pltpu.VMEM(normalizer.shape, F32),
            pltpu.VMEM((steps * rows, dk), F32),
            pltpu.SemaphoreType.DMA((7,)),
        ],
        compiler_params=LIMIT,
        cost_estimate=FREE,
        name="leave",
    )(slots, mask, memory, normalizer, queries.reshape(steps * rows, dk))


def hold_kernel(x, after, out):
    pass


def hold(x, after):
    return pl.pallas_call(
        hold_kernel,
        in_specs=[VMEM, ANY],
        out_specs=VMEM,
        out_shape=jax.ShapeDtypeStruct(x.shape, x.dtype),
        input_output_aliases={0: 0},
        compiler_params=LIMIT,
        cost_estimate=FREE,
        name="hold",
    )(x, after)


def answer_kernel(head, tail, asked, norms, after, out, tail_on):
    steps = asked.shape[0] // 2
    cut, dk = head.shape[0], asked.shape[1]
    q = asked[...].astype(BF16)
    dv = head.shape[1]
    out[:, dv:] = norms[...]
    first = lax.broadcasted_iota(jnp.int32, (2 * steps, 1), 0) < steps
    parts = ((head, 0, 0), (tail, 0, cut), (tail, dk - cut, 0), (tail, dk, cut))

    @pl.loop(0, dv // 256)
    def _(i):
        at = pl.ds(pl.multiple_of(i * 256, 256), 256)
        r = []
        for x, start, k in parts:
            high, low = halves(x[pl.ds(start, cut), at])
            r.append(dot(q[:, k : k + cut], high) + dot(q[:, k : k + cut], low))
        out[:, at] = jnp.where(first, r[0] + r[1], r[2] + r[3])


def answer(head, tail, asked, norms, after):
    return pl.pallas_call(
        answer_kernel,
        in_specs=[VMEM] * 5,
        out_specs=[VMEM, VMEM],
        out_shape=[
            pltpu.VMEM((asked.shape[0], head.shape[1] + asked.shape[1]), F32),
            jax.ShapeDtypeStruct(tail.shape, F32),
        ],
        input_output_aliases={1: 1},
        compiler_params=LIMIT,
        cost_estimate=FREE,
        name="answer",
    )(head, tail, asked, norms, after)


def weigh_kernel(igate, fgate, active, queries, keys, values, khat, decay, top, under, reach, token):
    token[...] = jnp.zeros_like(token)
    steps, rows, dk = keys.shape
    forget, inflow, _ = gates(igate, fgate, active)
    k = [keys[t].astype(F32) for t in range(steps)]
    weight = jnp.ones_like(forget[0])
    for t in reversed(range(steps)):
        khat[t] = (weight * inflow[t]) * k[t]
        weight = weight * forget[t]
    decay[...] = jnp.broadcast_to(weight, decay.shape)
    beta, so_far = [], jnp.ones_like(forget[0])
    for t in range(steps):
        q = queries[t].astype(F32) * (dk**-0.5)
        beta = [b * forget[t] for b in beta] + [inflow[t]]
        so_far = so_far * forget[t]
        above, below = 0.0, 0.0
        for s in range(t + 1):
            share = beta[s] * jnp.sum(k[s] * q, axis=1, keepdims=True)
            above = above + share * values[s].astype(F32)
            below = below + share
        top[t] = above
        under[t] = jnp.broadcast_to(below, under.shape[1:])
        reach[t] = jnp.broadcast_to(so_far * (dk**-0.5), reach.shape[1:])


def weigh(igate, fgate, active, queries, keys, values):
    steps, rows, dk = keys.shape
    dv = values.shape[2]
    shapes = ((steps, rows, dk), (rows, 128), (steps, rows, dv), (steps, rows, 128), (steps, rows, 128), (8, 128))
    return pl.pallas_call(
        weigh_kernel,
        in_specs=[VMEM] * 6,
        out_specs=[VMEM] * len(shapes),
        out_shape=[pltpu.VMEM(x, F32) for x in shapes],
        compiler_params=LIMIT,
        cost_estimate=FREE,
        name="weigh",
    )(igate, fgate, active, queries, keys, values)


def products_kernel(queries, memory, prod, wide_q):
    steps, rows, _ = queries.shape
    wide_q[...] = queries[...].astype(F32)

    @pl.loop(0, rows, unroll=2)
    def _(row):
        q = jnp.concatenate([wide_q[t, pl.ds(row, 1), :] for t in range(steps)], axis=0)
        q = jnp.concatenate([q, q], axis=0).astype(BF16)
        high, low = halves(memory[row])
        r = dot(q, high) + dot(q, low)
        for t in range(steps):
            prod[t, pl.ds(row, 1), :] = r[t : t + 1, :]


def products(queries, memory):
    steps, rows, dk = queries.shape
    return pl.pallas_call(
        products_kernel,
        in_specs=[VMEM] * 2,
        out_specs=VMEM,
        out_shape=pltpu.VMEM((steps, rows, memory.shape[2]), F32),
        scratch_shapes=[pltpu.VMEM((steps, rows, dk), F32)],
        compiler_params=LIMIT,
        cost_estimate=cost(PRODUCTS),
        name="products",
    )(queries, memory)


def update_kernel(slots, khat, decay, values, memory, head, normalizer, back, new, new_norm, add, keep, where, wide_v, done, norm_done, sems):
    steps, rows, dk = khat.shape
    dv, cut = values.shape[2], head.shape[0]
    width = 256
    wide_v[...] = values[...].astype(F32)
    for j in range(2):
        where[0, j] = slots[0, j]

    def leave(row):
        return pltpu.make_async_copy(done.at[row], new.at[row], sems.at[row])

    def terms(row):
        k = jnp.concatenate([khat[t, pl.ds(row, 1), :] for t in range(steps)], axis=0)
        k_high = k.astype(BF16).astype(F32)
        k = jnp.concatenate([k_high, k - k_high], axis=0).T.astype(BF16)
        v = jnp.concatenate([wide_v[t, pl.ds(row, 1), :] for t in range(steps)], axis=0)
        f = decay[pl.ds(row, 1), :]
        return k, jnp.concatenate([v, v], axis=0).astype(BF16), jnp.concatenate([f] * (dv // f.shape[1]), axis=1)

    index = lax.broadcasted_iota(jnp.int32, (rows, 1), 0)
    norm = jnp.concatenate([normalizer[b] for b in range(rows)], axis=0)
    for j in range(2):
        norm = jnp.where(index == slots[0, j], back[steps * j : steps * j + 1, dv:], norm)
    f = decay[...]
    norm = jnp.concatenate([f] * (dk // f.shape[1]), axis=1) * norm
    for t in range(steps):
        norm = norm + khat[t]
    for b in range(rows):
        norm_done[b] = norm[b : b + 1, :]
    norm_out = pltpu.make_async_copy(norm_done, new_norm, sems.at[rows])
    norm_out.start()

    @pl.loop(0, rows)
    def _(row):
        k, v, f = terms(row)
        for start in range(0, dv, width):
            at = pl.ds(start, width)
            done[row, :, at] = f[:, start : start + width] * memory[row, :, at] + dot(k, v[:, start : start + width])

        @pl.when(row == slots[0, 0])
        def _():
            done[row, 0:cut, :] = f * head[...] + dot(k[:cut], v)

        leave(row).start()

    k, v, f = terms(slots[0, 0])
    add[0 : dk - cut, :] = dot(k[cut:], v)
    keep[0:4, :] = jnp.concatenate([f] * 4, axis=0)
    k, v, f = terms(slots[0, 1])
    add[dk - cut :, :] = dot(k, v)
    keep[4:8, :] = jnp.concatenate([f] * 4, axis=0)
    norm_out.wait()
    for row in range(rows):
        leave(row).wait()


def update(slots, khat, decay, values, memory, head, normalizer, back):
    steps, rows, dk = khat.shape
    dv, tail = memory.shape[2], 2 * dk - head.shape[0]
    return pl.pallas_call(
        update_kernel,
        in_specs=[SMEM] + [VMEM] * 7,
        out_specs=[ANY, ANY, VMEM, VMEM, SMEM],
        out_shape=[
            pltpu.HBM(memory.shape, F32),
            pltpu.HBM(normalizer.shape, F32),
            pltpu.VMEM((tail, dv), F32),
            pltpu.VMEM((8, dv), F32),
            pltpu.SMEM(slots.shape, slots.dtype),
        ],
        scratch_shapes=[
            pltpu.VMEM(values.shape, F32),
            pltpu.VMEM(memory.shape, F32),
            pltpu.VMEM(normalizer.shape, F32),
            pltpu.SemaphoreType.DMA((rows + 1,)),
        ],
        compiler_params=LIMIT,
        cost_estimate=cost(UPDATE),
        name="update",
    )(slots, khat, decay, values, memory, head, normalizer, back)


def project_kernel(
    place, slots, active, queries, ogate, normalizer, prod, top, under, reach, back, weight, after,
    o0, o1, o2, o3, hidden,
):
    steps, rows, dk = queries.shape
    dv, cols = weight.shape[0], o0.shape[2]
    live = column((active[...] == 1).astype(F32)) > 0.0
    index = lax.broadcasted_iota(jnp.int32, (rows, 1), 0)
    moved = [index == slots[:, j : j + 1] for j in range(2)]
    norm = jnp.concatenate([normalizer[b] for b in range(rows)], axis=0)
    for j in range(2):
        norm = jnp.where(moved[j], back[steps * j : steps * j + 1, dv:], norm)
    for t in range(steps):
        cell = prod[t]
        for j in range(2):
            cell = jnp.where(moved[j], back[j * steps + t : j * steps + t + 1, :dv], cell)
        factor = reach[t]
        below = under[t] + factor * jnp.sum(norm * queries[t].astype(F32), axis=1, keepdims=True)
        below = jnp.maximum(jnp.abs(below), 1.0)
        factor, below = (jnp.concatenate([x] * (dv // x.shape[1]), axis=1) for x in (factor, below))
        out = (factor * cell + top[t]) / below * jax.nn.sigmoid(ogate[t].astype(F32))
        hidden[t * rows : (t + 1) * rows, :] = jnp.where(live, out, 0.0)

    h = hidden[...].astype(BF16)

    @pl.loop(0, 4)
    def _(m):
        r = []
        for p in range(2):
            at = pl.ds(pl.multiple_of(lax.bitwise_xor(place[0], 2 * m + p) * cols, cols), cols)
            r.append(dot(h, weight[:, at]))
        for n, out in enumerate((o0, o1, o2, o3)):

            @pl.when(m == n)
            def _(out=out):
                out[0] = r[0]
                out[1] = r[1]


def project(place, slots, active, queries, ogate, normalizer, prod, top, under, reach, back, weight, after):
    steps, rows, _ = queries.shape
    dv, width = weight.shape
    return pl.pallas_call(
        project_kernel,
        in_specs=[SMEM] + [VMEM] * 11 + [ANY],
        out_specs=[VMEM] * 4,
        out_shape=[pltpu.VMEM((2, steps * rows, width // 8), F32)] * 4,
        scratch_shapes=[pltpu.VMEM((steps * rows, dv), F32)],
        compiler_params=LIMIT,
        cost_estimate=FREE,
        name="project",
    )(place, slots, active, queries, ogate, normalizer, prod, top, under, reach, back, weight, after)


def merge_kernel(r2, r3, r1, o0, after, own, other):
    own[...] = o0[0] + r1[0] + (r2[0] + r3[0])
    other[...] = o0[1] + r1[1] + (r2[1] + r3[1])


def merge(r2, r3, r1, o0, after):
    return pl.pallas_call(
        merge_kernel,
        in_specs=[VMEM] * 4 + [ANY],
        out_specs=[VMEM] * 2,
        out_shape=[pltpu.VMEM(o0.shape[1:], F32)] * 2,
        compiler_params=LIMIT,
        cost_estimate=FREE,
        name="merge",
    )(r2, r3, r1, o0, after)


def finish_kernel(slots, tail, add, keep, tokens, own, z, former, new, mixed, done, mixed_done, sems):
    dk, rest = new.shape[1], new.shape[1] * 2 - tail.shape[0]
    outs = [pltpu.make_async_copy(mixed_done, mixed, sems.at[0])]
    mixed_done[...] = (tokens[...].astype(F32) + (own[...] + z[...])).astype(BF16)
    outs[0].start()
    size = rest
    for i in range(tail.shape[0] // size):
        j, row = divmod(i * size + dk - rest, dk)
        at = pl.ds(i * size, size)
        done[at, :] = keep[4 * j : 4 * j + 1, :] * tail[at, :] + add[at, :]
        outs.append(pltpu.make_async_copy(done.at[at], new.at[slots[0, j], pl.ds(row, size)], sems.at[1 + i]))
        outs[-1].start()
    for c in outs:
        c.wait()


def finish(slots, tail, add, keep, tokens, own, z, former):
    return pl.pallas_call(
        finish_kernel,
        in_specs=[SMEM] + [VMEM] * 6 + [ANY],
        out_specs=[ANY, ANY],
        out_shape=[pltpu.HBM(former.shape, F32), pltpu.HBM(tokens.shape, BF16)],
        scratch_shapes=[
            pltpu.VMEM(tail.shape, F32),
            pltpu.VMEM(tokens.shape, BF16),
            pltpu.SemaphoreType.DMA((1 + tail.shape[0] // (2 * former.shape[1] - tail.shape[0]),)),
        ],
        input_output_aliases={7: 0},
        compiler_params=LIMIT,
        cost_estimate=FREE,
        name="finish",
    )(slots, tail, add, keep, tokens, own, z, former)


def per_device(
    memory,
    normalizer,
    queries,
    keys,
    values,
    igate,
    fgate,
    ogate,
    out_weight,
    tokens,
    active,
    pair_mask,
    swap_slots,
):
    steps, rows = queries.shape[0], queries.shape[1]
    groups, heads = lax.axis_size("group"), lax.axis_size("head")
    memory = memory.reshape(rows, *memory.shape[2:])
    queries, keys, values, ogate = (x.reshape(steps, rows, x.shape[3]) for x in (queries, keys, values, ogate))
    igate, fgate = igate.reshape(steps, 1, rows), fgate.reshape(steps, 1, rows)
    active = active.reshape(1, rows)
    weight = out_weight.reshape(out_weight.shape[1:])
    place = lax.axis_index("head").astype(jnp.int32).reshape(1)
    head, tail, asked, norms, core, rest = leave(swap_slots, pair_mask, memory, normalizer, queries)

    def cores(*parts):
        return tuple(lax.ppermute(x, "group", [(s, s ^ 1) for s in range(groups)]) for x in parts)

    def stay(*parts):
        return parts

    def cores_head(head, tail, norms):
        head, norms = cores(head, norms)
        return head, tail, norms

    odd = core[0] == 1
    way = core[0] * (2 - jnp.where(rest[0] == 0, 1, lax.bitwise_and(rest[0], 1)))
    head, tail, norms = lax.switch(way, [stay, cores, cores_head], head, tail, norms)

    def branch(rest):
        def swap(x):
            return lax.ppermute(x, "group", [(s, s ^ (2 * rest)) for s in range(groups)]) if rest else x

        def across(x, bits):
            return lax.ppermute(x, "head", [(s, s ^ bits) for s in range(heads)])

        def run(*_):
            asked_in = swap(asked)
            first = hold(head, asked)
            head_in = swap(first)
            khat, decay, top, under, reach, token = weigh(igate, fgate, active, queries, keys, values)
            tail_here = tail
            if rest in (2, 4, 6):
                (tail_here,) = lax.cond(odd, cores, stay, hold(tail, token))
            reply, tail_on = answer(first, tail_here, asked_in, norms, token)
            back = swap(reply)
            tail_in = swap(tail_on)
            prod = products(queries, memory)
            o0, o1, o2, o3 = project(
                place, swap_slots, active, queries, ogate, normalizer, prod, top, under, reach, back, weight, head_in
            )
            r2, r3, r1 = across(o2, 4), across(o3, 6), across(o1, 2)
            new, new_norm, add, keep, where = update(swap_slots, khat, decay, values, memory, head_in, normalizer, back)
            own, beside = merge(r2, r3, r1, o0, new)
            z = across(beside, 1)
            new, mixed = finish(where, tail_in, add, keep, tokens.reshape(own.shape), own, z, new)
            return new, new_norm, mixed

        return run

    new, new_norm, mixed = lax.switch(rest[0], [branch(rest) for rest in range(groups // 2)])
    return new.reshape(rows, 1, *new.shape[1:]), new_norm, mixed.reshape(tokens.shape)


def solution(mesh):
    placed = (
        P("group", "head", None, None),
        P("group", "head", None),
        P(None, "group", "head", None),
        P(None, "group", "head", None),
        P(None, "group", "head", None),
        P(None, "group", "head"),
        P(None, "group", "head"),
        P(None, "group", "head", None),
        P("head", None, None),
        P(None, "group", "head"),
        P("group"),
        P(),
        P("group", None),
    )
    return jax.shard_map(
        per_device,
        mesh=mesh,
        in_specs=placed,
        out_specs=(
            P("group", "head", None, None),
            P("group", "head", None),
            P(None, "group", "head"),
        ),
        check_vma=False,
    )
```
